256 devices in a mesh: pipe: 4 (over y_hi, core), head: 16 (over z, y_lo), dp: 4 (over x).
Axes of the slice: x: 4, y: 4 (y_hi: 2, y_lo: 2; y = y_hi * 2 + y_lo), z: 8, core: 2. Of those that a mesh axis runs over, the one named last changes fastest.
Arguments:
- fwd_qkv: bfloat16 [4, 4, 1024, 3, 4096], P('dp', 'pipe', 'head'), may hold values from -6 to 6
- bwd_qkv: bfloat16 [4, 4, 1024, 3, 4096], P('dp', 'pipe', 'head'), may hold values from -6 to 6
- bwd_grad_out: bfloat16 [4, 4, 1024, 4096], P('dp', 'pipe', 'head'), may hold values from -6 to 6
- fwd_doc: int32 [4, 4, 1024], P('dp', 'pipe'), may hold values from 0 to 3, never falling along the last dimension, each value on 1 to 512 neighbouring positions
- bwd_doc: int32 [4, 4, 1024], P('dp', 'pipe'), may hold values from 0 to 3, never falling along the last dimension, each value on 1 to 512 neighbouring positions
- norm_gain: float32 [4, 2, 32, 128], replicated, may hold values from 0.6 to 5.5
- grad_acc: float32 [4, 4, 2, 2, 32, 128], P('dp', 'pipe', None, None, 'head'), may hold values from -96 to 96
Outputs:
- fwd_out: bfloat16 [4, 4, 1024, 4096], P('dp', 'pipe', 'head')
- bwd_qkv_grad: bfloat16 [4, 4, 1024, 3, 4096], P('dp', 'pipe', 'head')
- gain_grad: float32 [4, 2, 32, 128], P('pipe', None, 'head')
The draws below stay inside these ranges and needn't reach their ends.
Inputs may be any that keep to these rules, and one draw needn't show every extreme that they name: `fwd_doc`: document ids never fall along a sequence. `bwd_doc`: document ids never fall along a sequence.
All inputs are finite; a program needn't handle non-finite values.
Results may differ from the reference program's by a relative error of at most 0.013.
The reference program's roundings to bfloat16 on the way count: a program that leaves them out, or rounds other values in their place, can miss the bound.
Values may be sent and summed in bfloat16 or wider, within the bound.
No kernel may reach another device: no remote copies, remote signals or barrier semaphores. Data moves between devices by JAX's collectives and lax.ppermute only.
A program may use at most 64 MiB of HBM per device.

```python
import math
import jax
import jax.numpy as jnp
import numpy as np
from jax import lax

HEADS = 32
DH = 128
DOCS = 4
HD = 4096
SEQ = 1024
N_PIPE = 4
N_DP = 4


def draw_fwd_qkv(key, part):
    key = jax.random.fold_in(key, 11)
    shape = (N_DP, N_PIPE, SEQ, 3, HD)
    drawn = jax.random.normal(key, shape, jnp.float32)
    return jnp.clip(drawn, -6.0, 6.0).astype(jnp.bfloat16)


def draw_bwd_qkv(key, part):
    key = jax.random.fold_in(key, 12)
    shape = (N_DP, N_PIPE, SEQ, 3, HD)
    drawn = jax.random.normal(key, shape, jnp.float32)
    return jnp.clip(drawn, -6.0, 6.0).astype(jnp.bfloat16)


def draw_norm_gain(key, part):
    key = jax.random.fold_in(key, 13)
    shape = (N_PIPE, 2, HEADS, DH)
    return jax.random.uniform(key, shape, jnp.float32, 0.6, 1.6)


def steps_of(key, shape, split, smallest, high):
    level = 1.0
    for dim, blocks in split:
        heights = jax.random.uniform(jax.random.fold_in(jax.random.fold_in(key, 6), dim), (blocks,), jnp.float32, smallest / len(split), high / len(split))
        level = level * jnp.repeat(jnp.exp(heights), shape[dim] // blocks).reshape((-1,) + (1,) * (len(shape) - 1 - dim))
    return level


def length_profile(number_of, total, reach, lean):
    loads = [(1 << 20) // math.isqrt(grade ** lean) + 1 for grade in range(2, number_of + 1)]
    surplus, holding = total - reach - (number_of - 1), [1] * (number_of - 1)
    while surplus > 0:
        free = [i for i in range(number_of - 1) if holding[i] < reach]
        whole, budget = sum([loads[i] for i in free]), surplus
        for i in free:
            addition = min(reach - holding[i], max(1, budget * loads[i] // whole), surplus)
            holding[i] = holding[i] + addition
            surplus = surplus - addition
    return np.array([reach] + holding)


def uneven_parts(stream_key, number_of, total, bound, skew):
    if number_of == 2:
        one = jax.random.randint(stream_key, (), max(1, total - bound), min(bound, total - 1) + 1)
        return jnp.stack([one, total - one])
    sizes = jnp.asarray(length_profile(number_of, total, bound, skew), jnp.int32)
    twos = (number_of - 1) // 2
    giver, taker = sizes[1:1 + 2 * twos:2], sizes[2:2 + 2 * twos:2]
    room = jnp.minimum(giver - 1, bound - taker)
    passed = jax.random.randint(jax.random.fold_in(stream_key, 1), (twos,), 0, 1 << 20) % (room + 1)
    sizes = sizes.at[1:1 + 2 * twos:2].set(giver - passed).at[2:2 + 2 * twos:2].set(taker + passed)
    return sizes[jax.random.permutation(jax.random.fold_in(stream_key, 2), number_of)]


def gaussian(rng, extent, deviation, most, split=(), kind=jnp.bfloat16):
    array = deviation * jax.random.normal(rng, extent, jnp.float32)
    if split:
        array = array * steps_of(rng, extent, split, -0.22, 0.18)
    return jnp.clip(array, -most, most).astype(kind)


def setup_inputs(seed: int = 0) -> dict:
    streams_of = jax.random.split(jax.random.key(seed), 8)
    fwd_qkv = draw_fwd_qkv(jax.random.fold_in(streams_of[7], 71), 0)
    bwd_qkv = draw_bwd_qkv(jax.random.fold_in(streams_of[7], 71), 0)
    bwd_grad_out = gaussian(streams_of[2], (N_DP, N_PIPE, SEQ, HD), 1.0, 6.0, ((0, 4), (1, 4), (2, 16)))
    fwd_doc = jax.vmap(lambda own: jnp.searchsorted(jnp.cumsum(uneven_parts(own, DOCS, SEQ, SEQ // 2, 0)), jnp.arange(SEQ), side="right"))(jax.random.split(streams_of[3], N_DP * N_PIPE)).reshape((N_DP, N_PIPE, SEQ)).astype(jnp.int32)
    bwd_doc = jax.vmap(lambda own: jnp.searchsorted(jnp.cumsum(uneven_parts(own, DOCS, SEQ, SEQ // 2, 0)), jnp.arange(SEQ), side="right"))(jax.random.split(streams_of[4], N_DP * N_PIPE)).reshape((N_DP, N_PIPE, SEQ)).astype(jnp.int32)
    norm_gain = draw_norm_gain(jax.random.fold_in(streams_of[7], 71), 0)
    grad_acc = gaussian(streams_of[6], (N_DP, N_PIPE, 2, 2, HEADS, DH), 16.0, 96.0, ((0, 4), (1, 4), (4, 16)), jnp.float32)
    return dict(fwd_qkv=fwd_qkv, bwd_qkv=bwd_qkv, bwd_grad_out=bwd_grad_out, fwd_doc=fwd_doc, bwd_doc=bwd_doc, norm_gain=norm_gain, grad_acc=grad_acc)


EPS = 1e-06

def normalize(raw, gain):
    values = raw.astype(jnp.float32)
    recip = lax.rsqrt(lax.optimization_barrier(jnp.mean(values * values, axis=-1, keepdims=True)) + EPS)
    unit = values * recip
    return (unit, recip, (unit * gain).astype(jnp.bfloat16))

def block_probs(queries, keys, doc_rows, doc_cols, start):
    scale = 1.0 / math.sqrt(queries.shape[-1])
    scores = jnp.einsum('qhd,khd->hqk', queries.astype(jnp.float32), keys.astype(jnp.float32)) * scale
    rows = start + jnp.arange(queries.shape[0], dtype=jnp.int32)
    cols = jnp.arange(keys.shape[0], dtype=jnp.int32)
    allowed = (cols[None, :] <= rows[:, None]) & (doc_cols[None, :] == doc_rows[:, None])
    scores = jnp.where(allowed[None], scores, -jnp.inf)
    peak = lax.optimization_barrier(jnp.max(scores, axis=-1, keepdims=True))
    expo = jnp.exp(scores - peak)
    return expo / lax.optimization_barrier(jnp.sum(expo, axis=-1, keepdims=True))

def forward_heads(queries, keys, values, docs):
    length = queries.shape[0]
    block_rows = min(512, length)
    pieces = []
    for block in range(length // block_rows):
        start = block * block_rows
        finish = start + block_rows
        probs = block_probs(queries[start:finish], keys[:finish], docs[start:finish], docs[:finish], start).astype(jnp.bfloat16)
        result = jnp.einsum('hqk,khd->qhd', probs.astype(jnp.float32), values[:finish].astype(jnp.float32))
        pieces.append(result.astype(jnp.bfloat16))
    return jnp.concatenate(pieces, axis=0)

def backward_heads(queries, keys, values, upstream_all, docs):
    length = queries.shape[0]
    block_rows = min(512, length)
    scale = 1.0 / math.sqrt(queries.shape[-1])
    key_grad = jnp.zeros(queries.shape, jnp.float32)
    value_grad = jnp.zeros(queries.shape, jnp.float32)
    query_parts = []
    for block in range(length // block_rows):
        start = block * block_rows
        finish = start + block_rows
        probs = block_probs(queries[start:finish], keys[:finish], docs[start:finish], docs[:finish], start)
        rounded = probs.astype(jnp.bfloat16)
        outputs = jnp.einsum('hqk,khd->qhd', rounded.astype(jnp.float32), values[:finish].astype(jnp.float32))
        upstream = upstream_all[start:finish].astype(jnp.float32)
        dsum = lax.optimization_barrier(jnp.sum(upstream * outputs, axis=-1))
        dprob = jnp.einsum('qhd,khd->hqk', upstream, values[:finish].astype(jnp.float32))
        dscore = (probs * (dprob - dsum.T[:, :, None])).astype(jnp.bfloat16)
        query_parts.append((jnp.einsum('hqk,khd->qhd', dscore.astype(jnp.float32), keys[:finish].astype(jnp.float32)) * scale).astype(jnp.bfloat16))
        key_grad = key_grad.at[:finish].add(jnp.einsum('hqk,qhd->khd', dscore.astype(jnp.float32), queries[start:finish].astype(jnp.float32)) * scale)
        value_grad = value_grad.at[:finish].add(jnp.einsum('hqk,qhd->khd', rounded.astype(jnp.float32), upstream))
    return (jnp.concatenate(query_parts, axis=0), key_grad.astype(jnp.bfloat16), value_grad.astype(jnp.bfloat16))

def norm_back(grad_normed, unit, recip, gain):
    normed = grad_normed.astype(jnp.float32)
    scaled = normed * gain
    grad_in = recip * (scaled - unit * lax.optimization_barrier(jnp.mean(scaled * unit, axis=-1, keepdims=True)))
    return (grad_in.astype(jnp.bfloat16), lax.optimization_barrier(jnp.sum(normed * unit, axis=0)))

def reference(fwd_qkv, bwd_qkv, bwd_grad_out, fwd_doc, bwd_doc, norm_gain, grad_acc):
    pairs = N_DP * N_PIPE

    def one_pair(items):
        fwd_raw, bwd_raw, upstream, fwd_docs, bwd_docs, rank = items
        gain_down = norm_gain[rank]
        gain_up = norm_gain[N_PIPE - 1 - rank]
        fwd_raw = fwd_raw.reshape(SEQ, 3, HEADS, DH)
        bwd_raw = bwd_raw.reshape(SEQ, 3, HEADS, DH)
        fwd_query = normalize(fwd_raw[:, 0], gain_down[0])[2]
        fwd_key = normalize(fwd_raw[:, 1], gain_down[1])[2]
        attended = forward_heads(fwd_query, fwd_key, fwd_raw[:, 2], fwd_docs).reshape(SEQ, HD)
        query_unit, query_recip, bwd_query = normalize(bwd_raw[:, 0], gain_up[0])
        key_unit, key_recip, bwd_key = normalize(bwd_raw[:, 1], gain_up[1])
        query_normed, key_normed, value_grad = backward_heads(bwd_query, bwd_key, bwd_raw[:, 2], upstream.reshape(SEQ, HEADS, DH), bwd_docs)
        query_in, query_part = norm_back(query_normed, query_unit, query_recip, gain_up[0])
        key_in, key_part = norm_back(key_normed, key_unit, key_recip, gain_up[1])
        grads = jnp.stack([query_in, key_in, value_grad], axis=1).reshape(SEQ, 3, HD)
        return (attended, grads, jnp.stack([query_part, key_part]))
    ranks = jnp.tile(jnp.arange(N_PIPE, dtype=jnp.int32), N_DP)
    results = lax.map(one_pair, (fwd_qkv.reshape(pairs, SEQ, 3, HD), bwd_qkv.reshape(pairs, SEQ, 3, HD), bwd_grad_out.reshape(pairs, SEQ, HD), fwd_doc.reshape(pairs, SEQ), bwd_doc.reshape(pairs, SEQ), ranks))
    fwd_out = results[0].reshape(N_DP, N_PIPE, SEQ, HD)
    bwd_qkv_grad = results[1].reshape(N_DP, N_PIPE, SEQ, 3, HD)
    fresh = results[2].reshape(N_DP, N_PIPE, 2, HEADS, DH)
    gain_grad = lax.optimization_barrier(jnp.sum(grad_acc[:, :, 0] + grad_acc[:, ::-1, 1] + fresh[:, ::-1], axis=0))
    return (fwd_out, bwd_qkv_grad, gain_grad)
```

```python
import functools
import math

import jax
import jax.numpy as jnp
from jax import lax
from jax.experimental import pallas as pl
from jax.experimental.pallas import tpu as pltpu
from jax.sharding import PartitionSpec as P

EPS = 1e-06
LONGEST = 512
BLOCK = 128
NT = (((1,), (1,)), ((), ()))
NN = (((1,), (0,)), ((), ()))
F32 = jnp.float32
BF16 = jnp.bfloat16


def dot(left, right, dims=NN):
    return lax.dot_general(left, right, dims, preferred_element_type=F32)


def unit_of(raw):
    values = raw.astype(F32)
    recip = lax.rsqrt(jnp.mean(values * values, axis=-1, keepdims=True) + EPS)
    return values * recip, recip


def starts_of(docs):
    first = jnp.zeros(docs.shape, jnp.int32)
    for value in range(3):
        count = jnp.sum((docs == value).astype(jnp.int32))
        first = first + jnp.where(docs > value, count, 0)
    return first


def window(block):
    low = max(0, block * BLOCK - LONGEST)
    return low, (block + 1) * BLOCK


def probs_of(keys, query, start, low, high):
    scores = dot(keys, query, NT)
    factor = math.log2(math.e) / math.sqrt(query.shape[-1])
    rows = lax.broadcasted_iota(jnp.int32, (BLOCK, BLOCK), 0)
    cols = lax.broadcasted_iota(jnp.int32, (BLOCK, BLOCK), 1)
    pieces = []
    for at in range(low, high, BLOCK):
        piece = scores[at - low : at - low + BLOCK]
        allowed = rows >= start - at
        if at + BLOCK == high:
            allowed = allowed & (rows <= cols)
        pieces.append(jnp.where(allowed, piece, -1e30))
    peak = jnp.max(functools.reduce(jnp.maximum, pieces), axis=0, keepdims=True)
    pieces = [jnp.exp2((piece - peak) * factor) for piece in pieces]
    total = jnp.sum(functools.reduce(jnp.add, pieces), axis=0, keepdims=True)
    share = 1.0 / total
    return [piece * share for piece in pieces]


def flat(ref, kind, tokens, dim):
    return ref[:, kind].reshape(tokens, dim)


def forward_kernel(raw_ref, gain_ref, doc_ref, _, out_ref, query_ref, key_ref, value_t_ref):
    sources, _, rows, dim = raw_ref.shape
    tokens = sources * rows
    query_ref[...] = (unit_of(flat(raw_ref, 0, tokens, dim))[0] * gain_ref[0]).astype(BF16)
    key_ref[...] = (unit_of(flat(raw_ref, 1, tokens, dim))[0] * gain_ref[1]).astype(BF16)
    value_t_ref[...] = flat(raw_ref, 2, tokens, dim).T
    starts = starts_of(doc_ref[...])
    per = BLOCK // rows
    for block in range(tokens // BLOCK):
        low, high = window(block)
        query = query_ref[block * BLOCK : high]
        probs = probs_of(key_ref[low:high], query, starts[block : block + 1], low, high)
        probs = jnp.concatenate([piece.astype(BF16) for piece in probs], axis=0)
        result = dot(value_t_ref[:, low:high], probs).T.astype(BF16)
        out_ref[block * per : (block + 1) * per, 0] = result.reshape(per, rows, dim)


def norm_back(raw, grad, gain):
    unit, recip = unit_of(raw)
    normed = grad.astype(F32)
    scaled = normed * gain
    grad_in = recip * (scaled - unit * jnp.mean(scaled * unit, axis=-1, keepdims=True))
    return grad_in.astype(BF16), jnp.sum(normed * unit, axis=0, keepdims=True)


def backward_kernel(
    raw_ref, gain_ref, doc_ref, out_ref, new_ref,
    query_ref, key_ref, key_t_ref, value_t_ref, up_t_ref, probs_ref, dscore_ref,
):
    sources, _, rows, dim = raw_ref.shape
    tokens = sources * rows
    scale = 1.0 / math.sqrt(dim)
    query_ref[...] = (unit_of(flat(raw_ref, 0, tokens, dim))[0] * gain_ref[0]).astype(BF16)
    key = (unit_of(flat(raw_ref, 1, tokens, dim))[0] * gain_ref[1]).astype(BF16)
    key_ref[...] = key
    key_t_ref[...] = key.T
    value_t_ref[...] = flat(raw_ref, 2, tokens, dim).T
    up_t_ref[...] = flat(raw_ref, 3, tokens, dim).T
    starts = starts_of(doc_ref[...])
    per = BLOCK // rows
    blocks = tokens // BLOCK
    new_query = jnp.zeros((1, dim), F32)
    new_key = jnp.zeros((1, dim), F32)

    def part(kind, low, high):
        return raw_ref[low // rows : high // rows, kind].reshape(high - low, dim)

    for block in range(blocks):
        low, high = window(block)
        here = slice(block * BLOCK, high)
        query = query_ref[here]
        probs = probs_of(key_ref[low:high], query, starts[block : block + 1], low, high)
        rounded = jnp.concatenate([piece.astype(BF16) for piece in probs], axis=0)
        probs_ref[low:high, here] = rounded
        result_t = dot(value_t_ref[:, low:high], rounded)
        dsum = jnp.sum(up_t_ref[:, here].astype(F32) * result_t, axis=0, keepdims=True)
        dprob = dot(part(2, low, high), part(3, block * BLOCK, high), NT)
        dscore = jnp.concatenate(
            [
                (piece * (dprob[at * BLOCK : (at + 1) * BLOCK] - dsum)).astype(BF16)
                for at, piece in enumerate(probs)
            ],
            axis=0,
        )
        dscore_ref[low:high, here] = dscore
        grad = (dot(key_t_ref[:, low:high], dscore) * scale).T.astype(BF16)
        grad_in, new = norm_back(part(0, block * BLOCK, high), grad, gain_ref[0])
        new_query = new_query + new
        out_ref[block * per : (block + 1) * per, 0] = grad_in.reshape(per, rows, dim)

    for block in range(blocks):
        low = block * BLOCK
        high = min(tokens, low + BLOCK + LONGEST)
        here = slice(low, low + BLOCK)
        grad = (dot(dscore_ref[here, low:high], query_ref[low:high]) * scale).astype(BF16)
        grad_in, new = norm_back(part(1, low, low + BLOCK), grad, gain_ref[1])
        new_key = new_key + new
        out_ref[block * per : (block + 1) * per, 1] = grad_in.reshape(per, rows, dim)
        value_grad = dot(probs_ref[here, low:high], part(3, low, high)).astype(BF16)
        out_ref[block * per : (block + 1) * per, 2] = value_grad.reshape(per, rows, dim)
    new_ref[0] = new_query
    new_ref[1] = new_key


def pack_kernel(*refs):
    out_ref = refs[-1]
    at = 0
    for ref in refs[:-1]:
        kinds = ref.shape[0]
        out_ref[0, at : at + kinds] = ref[...]
        at += kinds


def pack(arrays, ranks):
    rows = arrays[0].shape[1]
    wide = arrays[0].shape[2] // ranks
    kinds = sum(array.shape[0] for array in arrays)
    return pl.pallas_call(
        pack_kernel,
        grid=(ranks,),
        in_specs=[
            pl.BlockSpec((array.shape[0], rows, wide), lambda at: (0, 0, at)) for array in arrays
        ],
        out_specs=pl.BlockSpec((1, kinds, rows, wide), lambda at: (at, 0, 0, 0)),
        out_shape=jax.ShapeDtypeStruct((ranks, kinds, rows, wide), arrays[0].dtype),
        name="pack",
    )(*arrays)


def unpack_kernel(in_ref, bwd_ref, fwd_ref):
    bwd_ref[...] = in_ref[0, 0:3]
    fwd_ref[...] = in_ref[0, 3]


def unpack(array):
    ranks, kinds, rows, wide = array.shape
    return pl.pallas_call(
        unpack_kernel,
        grid=(ranks,),
        in_specs=[pl.BlockSpec((1, kinds, rows, wide), lambda at: (at, 0, 0, 0))],
        out_specs=[
            pl.BlockSpec((kinds - 1, rows, wide), lambda at: (0, 0, at)),
            pl.BlockSpec((rows, wide), lambda at: (0, at)),
        ],
        out_shape=[
            jax.ShapeDtypeStruct((kinds - 1, rows, wide * ranks), array.dtype),
            jax.ShapeDtypeStruct((rows, wide * ranks), array.dtype),
        ],
        name="unpack",
    )(array)


VMEM_LIMIT = 48 * 1024 * 1024


def backward_call(raw, gain, docs):
    ranks, kinds, rows, wide = raw.shape
    dim = gain.shape[-1]
    heads = wide // dim
    tokens = ranks * rows
    return pl.pallas_call(
        backward_kernel,
        grid=(heads,),
        in_specs=[
            pl.BlockSpec((ranks, kinds, rows, dim), lambda at: (0, 0, 0, at)),
            pl.BlockSpec((2, None, 1, dim), lambda at: (0, at, 0, 0)),
            pl.BlockSpec(docs.shape, lambda at: (0, 0)),
        ],
        out_specs=[
            pl.BlockSpec((ranks, 3, rows, dim), lambda at: (0, 0, 0, at)),
            pl.BlockSpec((2, None, 1, dim), lambda at: (0, at, 0, 0)),
        ],
        out_shape=[
            jax.ShapeDtypeStruct((ranks, 4, rows, wide), raw.dtype),
            jax.ShapeDtypeStruct((2, heads, 1, dim), F32),
        ],
        scratch_shapes=[
            pltpu.VMEM((tokens, dim), BF16),
            pltpu.VMEM((tokens, dim), BF16),
            pltpu.VMEM((dim, tokens), BF16),
            pltpu.VMEM((dim, tokens), BF16),
            pltpu.VMEM((dim, tokens), BF16),
            pltpu.VMEM((tokens, tokens), BF16),
            pltpu.VMEM((tokens, tokens), BF16),
        ],
        compiler_params=pltpu.CompilerParams(vmem_limit_bytes=VMEM_LIMIT),
        cost_estimate=pl.CostEstimate(
            flops=12 * heads * tokens * tokens * dim // 2,
            bytes_accessed=heads * tokens * dim * 14,
            transcendentals=heads * tokens * tokens // 2,
        ),
        name="backward",
    )(raw, gain, docs)


def forward_call(raw, gain, docs, out):
    ranks, kinds, rows, wide = raw.shape
    dim = gain.shape[-1]
    heads = wide // dim
    tokens = ranks * rows
    return pl.pallas_call(
        forward_kernel,
        grid=(heads,),
        in_specs=[
            pl.BlockSpec((ranks, kinds, rows, dim), lambda at: (0, 0, 0, at)),
            pl.BlockSpec((2, None, 1, dim), lambda at: (0, at, 0, 0)),
            pl.BlockSpec(docs.shape, lambda at: (0, 0)),
            pl.BlockSpec(memory_space=pl.ANY),
        ],
        out_specs=pl.BlockSpec((ranks, 1, rows, dim), lambda at: (0, 3, 0, at)),
        out_shape=jax.ShapeDtypeStruct(out.shape, out.dtype),
        scratch_shapes=[
            pltpu.VMEM((tokens, dim), BF16),
            pltpu.VMEM((tokens, dim), BF16),
            pltpu.VMEM((dim, tokens), BF16),
        ],
        input_output_aliases={3: 0},
        compiler_params=pltpu.CompilerParams(vmem_limit_bytes=VMEM_LIMIT),
        cost_estimate=pl.CostEstimate(
            flops=4 * heads * tokens * tokens * dim // 2,
            bytes_accessed=heads * tokens * dim * 8,
            transcendentals=heads * tokens * tokens // 2,
        ),
        name="forward",
    )(raw, gain, docs, out)


def exchange(value):
    return lax.all_to_all(value, "head", split_axis=0, concat_axis=0, tiled=True)


def body(fwd_qkv, bwd_qkv, bwd_grad_out, fwd_doc, bwd_doc, norm_gain, grad_acc):
    ranks = lax.axis_size("head")
    pipe_count = lax.axis_size("pipe")
    pipe_at = lax.axis_index("pipe")
    head_at = lax.axis_index("head")
    tokens = fwd_qkv.shape[2]
    width = fwd_qkv.shape[4]
    dim = norm_gain.shape[3]
    local_heads = norm_gain.shape[2] // ranks

    def gain_of(section):
        part = lax.dynamic_slice(
            norm_gain, (section, 0, head_at * local_heads, 0), (1, 2, local_heads, dim)
        )
        return part.reshape(2, local_heads, 1, dim)

    gain_down = gain_of(pipe_at)
    gain_up = gain_of(pipe_count - 1 - pipe_at)
    fwd_docs = fwd_doc.reshape(-1, BLOCK)
    bwd_docs = bwd_doc.reshape(-1, BLOCK)
    fwd_raw = fwd_qkv.reshape(tokens, 3, width).transpose(1, 0, 2)
    bwd_raw = bwd_qkv.reshape(tokens, 3, width).transpose(1, 0, 2)
    upstream = bwd_grad_out.reshape(1, tokens, width)

    bwd_group = exchange(pack([bwd_raw, upstream], ranks))
    fwd_group = exchange(pack([fwd_raw], ranks))
    grads, new = backward_call(bwd_group, gain_up, bwd_docs)
    results = forward_call(fwd_group, gain_down, fwd_docs, grads)
    returned = exchange(results)
    qkv_grad, fwd_out = unpack(returned)

    accum = grad_acc.reshape(2, 2, local_heads, dim)
    up_local = accum[1] + new.reshape(2, local_heads, dim)
    mirrored = lax.ppermute(up_local, "pipe", [(at, pipe_count - 1 - at) for at in range(pipe_count)])
    total = lax.psum(accum[0] + mirrored, "dp")
    return (
        fwd_out.reshape(1, 1, tokens, width),
        qkv_grad.transpose(1, 0, 2).reshape(1, 1, tokens, 3, width),
        total.reshape(1, 2, local_heads, dim),
    )


def solution(mesh):
    in_specs = (
        P("dp", "pipe", "head", None, None),
        P("dp", "pipe", "head", None, None),
        P("dp", "pipe", "head", None),
        P("dp", "pipe", None),
        P("dp", "pipe", None),
        P(),
        P("dp", "pipe", None, None, "head", None),
    )
    out_specs = (
        P("dp", "pipe", "head", None),
        P("dp", "pipe", "head", None, None),
        P("pipe", None, "head", None),
    )
    return jax.shard_map(body, mesh=mesh, in_specs=in_specs, out_specs=out_specs, check_vma=False)
```

```python
import functools
import math

import jax
import jax.numpy as jnp
from jax import lax
from jax.experimental import pallas as pl
from jax.experimental.pallas import tpu as pltpu
from jax.sharding import PartitionSpec as P

EPS = 1e-06
LONGEST = 512
BLOCK = 128
NT = (((1,), (1,)), ((), ()))
NN = (((1,), (0,)), ((), ()))
F32 = jnp.float32
BF16 = jnp.bfloat16


def dot(left, right, dims=NN):
    return lax.dot_general(left, right, dims, preferred_element_type=F32)


def unit_of(raw):
    values = raw.astype(F32)
    recip = lax.rsqrt(jnp.mean(values * values, axis=-1, keepdims=True) + EPS)
    return values * recip, recip


def starts_of(docs):
    first = jnp.zeros(docs.shape, jnp.int32)
    for value in range(3):
        count = jnp.sum((docs == value).astype(jnp.int32))
        first = first + jnp.where(docs > value, count, 0)
    return first


def window(block):
    low = max(0, block * BLOCK - LONGEST)
    return low, (block + 1) * BLOCK


def probs_of(keys, query, start, low, high):
    scores = dot(keys, query, NT)
    factor = math.log2(math.e) / math.sqrt(query.shape[-1])
    rows = lax.broadcasted_iota(jnp.int32, (BLOCK, BLOCK), 0)
    cols = lax.broadcasted_iota(jnp.int32, (BLOCK, BLOCK), 1)
    pieces = []
    for at in range(low, high, BLOCK):
        piece = scores[at - low : at - low + BLOCK]
        allowed = rows >= start - at
        if at + BLOCK == high:
            allowed = allowed & (rows <= cols)
        pieces.append(jnp.where(allowed, piece, -1e30))
    peak = jnp.max(functools.reduce(jnp.maximum, pieces), axis=0, keepdims=True)
    pieces = [jnp.exp2((piece - peak) * factor) for piece in pieces]
    total = jnp.sum(functools.reduce(jnp.add, pieces), axis=0, keepdims=True)
    share = 1.0 / total
    return [piece * share for piece in pieces]


def flat(ref, kind):
    ranks, _, rows, dim = ref.shape
    return ref[:, kind].reshape(ranks * rows, dim)


def load_pieces(pieces, group_ref, raw_refs, sems):
    kinds = raw_refs.shape[2]
    loads = [
        pltpu.make_async_copy(group_ref.at[:, first : first + kinds], raw_refs.at[slot], sems.at[slot])
        for slot, (_, first) in enumerate(pieces)
    ]
    for load in loads:
        load.start()
    return loads


def store_kinds(result_ref, out_ref, first, count, sem):
    store = pltpu.make_async_copy(
        result_ref.at[:, first : first + count], out_ref.at[:, first : first + count], sem
    )
    store.start()
    return store


def forward_kernel(
    pieces, group_ref, gain_ref, doc_ref, out_ref,
    raw_refs, result_ref, load_sems, store_sems, query_ref, key_ref, value_t_ref,
):
    loads = load_pieces(pieces, group_ref, raw_refs, load_sems)
    stores = []
    rows, dim = group_ref.shape[2:]
    starts = starts_of(doc_ref[...])
    per = BLOCK // rows
    for slot, (head, _) in enumerate(pieces):
        loads[slot].wait()
        raw_ref = raw_refs.at[slot]
        gain = gain_ref[:, head]
        query_ref[slot] = (unit_of(flat(raw_ref, 0))[0] * gain[0]).astype(BF16)
        key_ref[slot] = (unit_of(flat(raw_ref, 1))[0] * gain[1]).astype(BF16)
        value_t_ref[slot] = flat(raw_ref, 2).T
        for block in range(query_ref.shape[1] // BLOCK):
            low, high = window(block)
            query = query_ref[slot, block * BLOCK : high]
            probs = probs_of(key_ref[slot, low:high], query, starts[block : block + 1], low, high)
            probs = jnp.concatenate([piece.astype(BF16) for piece in probs], axis=0)
            result = dot(value_t_ref[slot, :, low:high], probs).T.astype(BF16)
            result_ref[block * per : (block + 1) * per, slot] = result.reshape(per, rows, dim)
        stores.append(store_kinds(result_ref, out_ref, slot, 1, store_sems.at[slot, 0]))
    for store in stores:
        store.wait()


def norm_back(raw, grad, gain):
    unit, recip = unit_of(raw)
    normed = grad.astype(F32)
    scaled = normed * gain
    grad_in = recip * (scaled - unit * jnp.mean(scaled * unit, axis=-1, keepdims=True))
    return grad_in.astype(BF16), jnp.sum(normed * unit, axis=0, keepdims=True)


def backward_kernel(
    pieces, group_ref, gain_ref, doc_ref, out_ref, new_ref,
    raw_refs, result_ref, load_sems, store_sems, query_refs, key_refs, key_t_refs, value_t_refs, up_t_refs, probs_refs, dscore_refs,
):
    loads = load_pieces(pieces, group_ref, raw_refs, load_sems)
    stores = []
    rows, dim = group_ref.shape[2:]
    tokens = query_refs.shape[1]
    scale = 1.0 / math.sqrt(dim)
    starts = starts_of(doc_ref[...])
    per = BLOCK // rows
    blocks = tokens // BLOCK

    for slot, (head, _) in enumerate(pieces):
        loads[slot].wait()
        query_ref, key_ref, key_t_ref, value_t_ref, up_t_ref, probs_ref, dscore_ref = [
            refs.at[slot]
            for refs in (
                query_refs, key_refs, key_t_refs, value_t_refs, up_t_refs, probs_refs, dscore_refs
            )
        ]
        gain = gain_ref[:, head]
        kind_out = 3 * slot

        def part(kind, low, high, raw_ref=raw_refs.at[slot]):
            piece = raw_ref[low // rows : high // rows, kind]
            return piece.reshape(high - low, dim)

        query_ref[...] = (unit_of(part(0, 0, tokens))[0] * gain[0]).astype(BF16)
        key = (unit_of(part(1, 0, tokens))[0] * gain[1]).astype(BF16)
        key_ref[...] = key
        key_t_ref[...] = key.T
        value_t_ref[...] = part(2, 0, tokens).T
        up_t_ref[...] = part(3, 0, tokens).T
        new_query = jnp.zeros((1, dim), F32)
        new_key = jnp.zeros((1, dim), F32)
        for block in range(blocks):
            low, high = window(block)
            here = slice(block * BLOCK, high)
            span = slice(block * per, (block + 1) * per)
            query = query_ref[here]
            probs = probs_of(key_ref[low:high], query, starts[block : block + 1], low, high)
            rounded = jnp.concatenate([piece.astype(BF16) for piece in probs], axis=0)
            probs_ref[low:high, here] = rounded
            result_t = dot(value_t_ref[:, low:high], rounded)
            dsum = jnp.sum(up_t_ref[:, here].astype(F32) * result_t, axis=0, keepdims=True)
            dprob = dot(part(2, low, high), part(3, block * BLOCK, high), NT)
            dscore = jnp.concatenate(
                [
                    (piece * (dprob[at * BLOCK : (at + 1) * BLOCK] - dsum)).astype(BF16)
                    for at, piece in enumerate(probs)
                ],
                axis=0,
            )
            dscore_ref[low:high, here] = dscore
            grad = (dot(key_t_ref[:, low:high], dscore) * scale).T.astype(BF16)
            grad_in, new = norm_back(part(0, block * BLOCK, high), grad, gain[0])
            new_query = new_query + new
            result_ref[span, kind_out] = grad_in.reshape(per, rows, dim)
        stores.append(store_kinds(result_ref, out_ref, kind_out, 1, store_sems.at[slot, 0]))

        for block in range(blocks):
            low = block * BLOCK
            high = min(tokens, low + BLOCK + LONGEST)
            here = slice(low, low + BLOCK)
            span = slice(block * per, (block + 1) * per)
            grad = (dot(dscore_ref[here, low:high], query_ref[low:high]) * scale).astype(BF16)
            grad_in, new = norm_back(part(1, low, low + BLOCK), grad, gain[1])
            new_key = new_key + new
            result_ref[span, kind_out + 1] = grad_in.reshape(per, rows, dim)
            value_grad = dot(probs_ref[here, low:high], part(3, low, high)).astype(BF16)
            result_ref[span, kind_out + 2] = value_grad.reshape(per, rows, dim)
        stores.append(store_kinds(result_ref, out_ref, kind_out + 1, 2, store_sems.at[slot, 1]))
        new_ref[0, head] = new_query
        new_ref[1, head] = new_key
    for store in stores:
        store.wait()


ANYWHERE = pl.BlockSpec(memory_space=pl.ANY)
IN_VMEM = pl.BlockSpec(memory_space=pltpu.VMEM)
VMEM_LIMIT = 40 * 1024 * 1024
KINDS_IN = {"f": 3, "b": 4}
KINDS_OUT = {"f": 1, "b": 3}


def places(pieces, kinds):
    found, at = {}, 0
    for piece in pieces:
        found[piece] = at
        at += kinds[piece[0]]
    return found, at


def wait_all(copies):
    for copy in copies:
        copy.start()
    for copy in copies:
        copy.wait()


def pack_kernel(pieces, ranks, *refs):
    *in_refs, out_ref, held_ref, load_sems, store_sems = refs
    dim = out_ref.shape[-1]
    heads = held_ref.shape[2] // (ranks * dim)
    loads, at = [], 0
    for index, ref in enumerate(in_refs):
        kinds = ref.shape[0]
        loads.append(pltpu.make_async_copy(ref, held_ref.at[at : at + kinds], load_sems.at[index]))
        loads[-1].start()
        at += kinds
    spans, at, index = {}, 0, 0
    stores, slot = [], 0
    for number, (name, head) in enumerate(pieces):
        if name not in spans:
            spans[name] = at
            for _ in range(1 if name == "f" else 2):
                loads[index].wait()
                index += 1
            at += KINDS_IN[name]
        kinds = KINDS_IN[name]
        for rank in range(ranks):
            low = (rank * heads + head) * dim
            store = pltpu.make_async_copy(
                held_ref.at[spans[name] : spans[name] + kinds, :, low : low + dim],
                out_ref.at[rank, slot : slot + kinds],
                store_sems.at[number, rank],
            )
            store.start()
            stores.append(store)
        slot += kinds
    for store in stores:
        store.wait()


def pack(sources, pieces, ranks, dim):
    names = list(dict.fromkeys(name for name, _ in pieces))
    arrays = [array for name in names for array in sources[name]]
    rows, width = arrays[0].shape[1:]
    held = sum(array.shape[0] for array in arrays)
    kinds = places(pieces, KINDS_IN)[1]
    return pl.pallas_call(
        functools.partial(pack_kernel, pieces, ranks),
        in_specs=[ANYWHERE] * len(arrays),
        out_specs=ANYWHERE,
        out_shape=pltpu.HBM((ranks, kinds, rows, dim), arrays[0].dtype),
        scratch_shapes=[
            pltpu.VMEM((held, rows, width), arrays[0].dtype),
            pltpu.SemaphoreType.DMA((len(arrays),)),
            pltpu.SemaphoreType.DMA((len(pieces), ranks)),
        ],
        compiler_params=pltpu.CompilerParams(vmem_limit_bytes=VMEM_LIMIT),
        name="pack",
    )(*[pltpu.with_memory_space_constraint(array, pltpu.HBM) for array in arrays])


def unpack_kernel(count, in_ref, out_ref, sems):
    ranks, _, _, dim = in_ref.shape
    kinds = out_ref.shape[0]
    copies = []
    for head in range(count):
        for rank in range(ranks):
            low = (rank * count + head) * dim
            copies.append(
                pltpu.make_async_copy(
                    in_ref.at[rank, head * kinds : (head + 1) * kinds],
                    out_ref.at[:, :, low : low + dim],
                    sems.at[head, rank],
                )
            )
    wait_all(copies)


def unpack(array, heads):
    ranks, kinds, rows, dim = array.shape
    return pl.pallas_call(
        functools.partial(unpack_kernel, heads),
        in_specs=[ANYWHERE],
        out_specs=ANYWHERE,
        out_shape=pltpu.HBM((kinds // heads, rows, ranks * heads * dim), array.dtype),
        scratch_shapes=[pltpu.SemaphoreType.DMA((heads, ranks))],
        compiler_params=pltpu.CompilerParams(vmem_limit_bytes=VMEM_LIMIT),
        name="unpack",
    )(array)


def attend(name, group, pieces, gain, docs):
    ranks, _, rows, dim = group.shape
    tokens = ranks * rows
    count = len(pieces)
    row_major = pltpu.VMEM((count, tokens, dim), BF16)
    col_major = pltpu.VMEM((count, dim, tokens), BF16)
    square = pltpu.VMEM((count, tokens, tokens), BF16)
    kinds_in, kinds_out = KINDS_IN[name], KINDS_OUT[name] * count
    scratch = [
        pltpu.VMEM((count, ranks, kinds_in, rows, dim), BF16),
        pltpu.VMEM((ranks, kinds_out, rows, dim), BF16),
        pltpu.SemaphoreType.DMA((count,)),
        pltpu.SemaphoreType.DMA((count, 2)),
        row_major,
        row_major,
        col_major,
    ]
    out_shape = [pltpu.HBM((ranks, kinds_out, rows, dim), group.dtype)]
    if name == "b":
        scratch += [col_major, col_major, square, square]
        out_shape.append(jax.ShapeDtypeStruct(gain.shape, F32))
    dots = 2 if name == "f" else 6
    return pl.pallas_call(
        functools.partial(forward_kernel if name == "f" else backward_kernel, pieces),
        in_specs=[ANYWHERE, IN_VMEM, IN_VMEM],
        out_specs=[ANYWHERE, IN_VMEM][: len(out_shape)],
        out_shape=out_shape,
        scratch_shapes=scratch,
        compiler_params=pltpu.CompilerParams(vmem_limit_bytes=VMEM_LIMIT),
        cost_estimate=pl.CostEstimate(
            flops=count * dots * tokens * tokens * dim,
            bytes_accessed=count * tokens * dim * 2 * (KINDS_IN[name] + KINDS_OUT[name]),
            transcendentals=count * tokens * tokens // 2,
        ),
        name="forward" if name == "f" else "backward",
    )(pltpu.with_memory_space_constraint(group, pltpu.HBM), gain, docs)


def exchange(value):
    return lax.all_to_all(value, "head", split_axis=0, concat_axis=0, tiled=True)


def after(value, earlier):
    return value if earlier is None else lax.optimization_barrier((value, earlier))[0]


F0, F1, B0, B1 = ("f", 0), ("f", 1), ("b", 0), ("b", 1)
PLANS = (
    (((B0, B1, F0, F1),), ("f", "b")),
    (((B0, B1), (F0, F1)), ("b", "f")),
)
TAIL = False


def branch(plan, fwd_raw, bwd_raw, upstream, gain_down, gain_up, fwd_docs, bwd_docs, accum):
    ranks = lax.axis_size("head")
    dim = gain_down.shape[-1]
    sources = {"f": [fwd_raw], "b": [bwd_raw, upstream]}
    gains = {"f": gain_down, "b": gain_up}
    docs = {"f": fwd_docs, "b": bwd_docs}
    ins, outs = plan
    latest, where = None, {}
    for pieces in ins:
        latest = exchange(after(pack(sources, pieces, ranks, dim), latest))
        for (name, head), first in places(pieces, KINDS_IN)[0].items():
            where.setdefault(name, (latest, []))[1].append((head, first))
    held, earlier = {}, None
    for index, name in enumerate(outs):
        group, pieces = where[name]
        results, *new = attend(name, after(group, earlier), tuple(pieces), gains[name], docs[name])
        if new:
            total = accum + jnp.stack([jnp.zeros_like(accum[0]), new[0].reshape(accum[0].shape)])
        earlier = results
        held[name] = after(results, latest)
        if not TAIL or index + 1 < len(outs):
            latest = exchange(held[name])
            held[name] = unpack(latest, 2)
    sums = lax.psum(total, "dp")
    return held["b"], held["f"], lax.optimization_barrier(sums)


def body(fwd_qkv, bwd_qkv, bwd_grad_out, fwd_doc, bwd_doc, norm_gain, grad_acc):
    ranks = lax.axis_size("head")
    pipe_count = lax.axis_size("pipe")
    pipe_at = lax.axis_index("pipe")
    head_at = lax.axis_index("head")
    tokens = fwd_qkv.shape[2]
    width = fwd_qkv.shape[4]
    dim = norm_gain.shape[3]
    local_heads = norm_gain.shape[2] // ranks

    def gain_of(section):
        part = lax.dynamic_slice(
            norm_gain, (section, 0, head_at * local_heads, 0), (1, 2, local_heads, dim)
        )
        return part.reshape(2, local_heads, 1, dim)

    args = (
        fwd_qkv.reshape(tokens, 3, width).transpose(1, 0, 2),
        bwd_qkv.reshape(tokens, 3, width).transpose(1, 0, 2),
        bwd_grad_out.reshape(1, tokens, width),
        gain_of(pipe_at),
        gain_of(pipe_count - 1 - pipe_at),
        fwd_doc.reshape(-1, BLOCK),
        bwd_doc.reshape(-1, BLOCK),
        grad_acc.reshape(2, 2, local_heads, dim),
    )
    qkv_grad, fwd_out, sums = lax.cond(
        pipe_at % 2 == 0,
        functools.partial(branch, PLANS[0]),
        functools.partial(branch, PLANS[1]),
        *args,
    )
    if TAIL:
        if PLANS[0][1][-1] == "f":
            fwd_out = unpack(exchange(fwd_out), local_heads)
        else:
            qkv_grad = unpack(exchange(qkv_grad), local_heads)
    mirrored = lax.ppermute(sums[1], "pipe", [(at, pipe_count - 1 - at) for at in range(pipe_count)])
    return (
        fwd_out.reshape(1, 1, tokens, width),
        qkv_grad.transpose(1, 0, 2).reshape(1, 1, tokens, 3, width),
        (sums[0] + mirrored).reshape(1, 2, local_heads, dim),
    )


def solution(mesh):
    in_specs = (
        P("dp", "pipe", "head", None, None),
        P("dp", "pipe", "head", None, None),
        P("dp", "pipe", "head", None),
        P("dp", "pipe", None),
        P("dp", "pipe", None),
        P(),
        P("dp", "pipe", None, None, "head", None),
    )
    out_specs = (
        P("dp", "pipe", "head", None),
        P("dp", "pipe", "head", None, None),
        P("pipe", None, "head", None),
    )
    return jax.shard_map(body, mesh=mesh, in_specs=in_specs, out_specs=out_specs, check_vma=False)
```

```python
import functools
import math

import jax
import jax.numpy as jnp
from jax import lax
from jax.experimental import pallas as pl
from jax.experimental.pallas import tpu as pltpu
from jax.sharding import PartitionSpec as P

EPS = 1e-06
LONGEST = 512
BLOCK = 128
NT = (((1,), (1,)), ((), ()))
NN = (((1,), (0,)), ((), ()))
F32 = jnp.float32
BF16 = jnp.bfloat16


def dot(left, right, dims=NN):
    return lax.dot_general(left, right, dims, preferred_element_type=F32)


def unit_of(raw):
    values = raw.astype(F32)
    recip = lax.rsqrt(jnp.mean(values * values, axis=-1, keepdims=True) + EPS)
    return values * recip, recip


def starts_of(docs):
    first = jnp.zeros(docs.shape, jnp.int32)
    for value in range(3):
        count = jnp.sum((docs == value).astype(jnp.int32))
        first = first + jnp.where(docs > value, count, 0)
    return first


def window(block):
    low = max(0, block * BLOCK - LONGEST)
    return low, (block + 1) * BLOCK


FORWARD_GROUP, BACKWARD_GROUP, KEY_GROUP = 8, 4, 4


def groups_of(count, blocks, size):
    items = [(slot, block) for block in range(blocks) for slot in range(count)]
    return [items[at : at + size] for at in range(0, len(items), size)]


def probs_of(scores, starts, spans, dim):
    factor = math.log2(math.e) / math.sqrt(dim)
    rows = lax.broadcasted_iota(jnp.int32, (BLOCK, BLOCK), 0)
    cols = lax.broadcasted_iota(jnp.int32, (BLOCK, BLOCK), 1)
    lists = []
    for score, start, (low, high) in zip(scores, starts, spans):
        pieces = []
        for at in range(low, high, BLOCK):
            allowed = rows >= start - at
            if at + BLOCK == high:
                allowed = allowed & (rows <= cols)
            pieces.append(jnp.where(allowed, score[at - low : at - low + BLOCK], -1e30))
        lists.append(pieces)
    peaks = [
        jnp.max(functools.reduce(jnp.maximum, pieces), axis=0, keepdims=True) for pieces in lists
    ]
    lists = [
        [jnp.exp2((piece - peak) * factor) for piece in pieces] for pieces, peak in zip(lists, peaks)
    ]
    shares = [
        1.0 / jnp.sum(functools.reduce(jnp.add, pieces), axis=0, keepdims=True) for pieces in lists
    ]
    return [[piece * share for piece in pieces] for pieces, share in zip(lists, shares)]


def flat(ref, kind):
    ranks, _, rows, dim = ref.shape
    return ref[:, kind].reshape(ranks * rows, dim)


def load_pieces(pieces, group_ref, raw_refs, sems):
    kinds = raw_refs.shape[2]
    loads = [
        pltpu.make_async_copy(group_ref.at[:, first : first + kinds], raw_refs.at[slot], sems.at[slot])
        for slot, (_, first) in enumerate(pieces)
    ]
    for load in loads:
        load.start()
    return loads


def store_kinds(result_ref, out_ref, base, first, count, sem):
    out_part = out_ref.at[:, base + first : base + first + count]
    store = pltpu.make_async_copy(result_ref.at[:, first : first + count], out_part, sem)
    store.start()
    return store


def forward_kernel(pieces, base, group_ref, gain_ref, doc_ref, *refs):
    (
        out_ref, raw_refs, result_ref, load_sems, store_sems, query_ref, key_ref, value_t_ref,
    ) = refs[-8:]
    loads = load_pieces(pieces, group_ref, raw_refs, load_sems)
    rows, dim = group_ref.shape[2:]
    starts = starts_of(doc_ref[...])
    per = BLOCK // rows
    for slot, (head, _) in enumerate(pieces):
        loads[slot].wait()
        raw_ref = raw_refs.at[slot]
        gain = gain_ref[:, head]
        query_ref[slot] = (unit_of(flat(raw_ref, 0))[0] * gain[0]).astype(BF16)
        key_ref[slot] = (unit_of(flat(raw_ref, 1))[0] * gain[1]).astype(BF16)
        value_t_ref[slot] = flat(raw_ref, 2).T
    for items in groups_of(len(pieces), query_ref.shape[1] // BLOCK, FORWARD_GROUP):
        spans = [window(block) for _, block in items]
        scores = [
            dot(key_ref[slot, low:high], query_ref[slot, block * BLOCK : high], NT)
            for (slot, block), (low, high) in zip(items, spans)
        ]
        probs = probs_of(scores, [starts[block : block + 1] for _, block in items], spans, dim)
        probs = [jnp.concatenate([piece.astype(BF16) for piece in every], axis=0) for every in probs]
        results = [
            dot(value_t_ref[slot, :, low:high], prob)
            for (slot, _), (low, high), prob in zip(items, spans, probs)
        ]
        for (slot, block), result in zip(items, results):
            result = result.T.astype(BF16).reshape(per, rows, dim)
            result_ref[block * per : (block + 1) * per, slot] = result
    store_kinds(result_ref, out_ref, base, 0, len(pieces), store_sems.at[0, 0]).wait()


def norm_back(raw, grad, gain):
    unit, recip = unit_of(raw)
    normed = grad.astype(F32)
    scaled = normed * gain
    grad_in = recip * (scaled - unit * jnp.mean(scaled * unit, axis=-1, keepdims=True))
    return grad_in.astype(BF16), jnp.sum(normed * unit, axis=0, keepdims=True)


def backward_kernel(pieces, base, group_ref, gain_ref, doc_ref, *refs):
    (
        out_ref, new_ref, raw_refs, result_ref, load_sems, store_sems,
        query_refs, key_refs, key_t_refs, value_t_refs, up_t_refs, probs_refs, dscore_refs,
    ) = refs[-13:]
    loads = load_pieces(pieces, group_ref, raw_refs, load_sems)
    rows, dim = group_ref.shape[2:]
    tokens = query_refs.shape[1]
    scale = 1.0 / math.sqrt(dim)
    starts = starts_of(doc_ref[...])
    per = BLOCK // rows
    blocks = tokens // BLOCK
    count = len(pieces)

    def part(slot, kind, low, high):
        return raw_refs[slot, low // rows : high // rows, kind].reshape(high - low, dim)

    for slot, (head, _) in enumerate(pieces):
        loads[slot].wait()
        gain = gain_ref[:, head]
        query_refs[slot] = (unit_of(part(slot, 0, 0, tokens))[0] * gain[0]).astype(BF16)
        key = (unit_of(part(slot, 1, 0, tokens))[0] * gain[1]).astype(BF16)
        key_refs[slot] = key
        key_t_refs[slot] = key.T
        value_t_refs[slot] = part(slot, 2, 0, tokens).T
        up_t_refs[slot] = part(slot, 3, 0, tokens).T
    new_query = [jnp.zeros((1, dim), F32)] * count
    new_key = [jnp.zeros((1, dim), F32)] * count
    for items in groups_of(count, blocks, BACKWARD_GROUP):
        spans = [window(block) for _, block in items]
        heres = [slice(block * BLOCK, (block + 1) * BLOCK) for _, block in items]
        every = [(slot, low, high, here) for (slot, _), (low, high), here in zip(items, spans, heres)]
        scores = [
            dot(key_refs[slot, low:high], query_refs[slot, here], NT) for slot, low, high, here in every
        ]
        dprobs = [
            dot(part(slot, 2, low, high), part(slot, 3, here.start, here.stop), NT)
            for slot, low, high, here in every
        ]
        probs = probs_of(scores, [starts[block : block + 1] for _, block in items], spans, dim)
        rounded = [jnp.concatenate([piece.astype(BF16) for piece in some], axis=0) for some in probs]
        results = [
            dot(value_t_refs[slot, :, low:high], some)
            for (slot, low, high, _), some in zip(every, rounded)
        ]
        for (slot, low, high, here), some in zip(every, rounded):
            probs_refs[slot, low:high, here] = some
        dsums = [
            jnp.sum(up_t_refs[slot, :, here].astype(F32) * result, axis=0, keepdims=True)
            for (slot, _, _, here), result in zip(every, results)
        ]
        dscores = [
            jnp.concatenate(
                [
                    (piece * (dprob[at * BLOCK : (at + 1) * BLOCK] - dsum)).astype(BF16)
                    for at, piece in enumerate(some)
                ],
                axis=0,
            )
            for some, dprob, dsum in zip(probs, dprobs, dsums)
        ]
        grads = [
            dot(key_t_refs[slot, :, low:high], dscore) * scale
            for (slot, low, high, _), dscore in zip(every, dscores)
        ]
        for (slot, low, high, here), dscore in zip(every, dscores):
            dscore_refs[slot, low:high, here] = dscore
        grads = [grad.T.astype(BF16) for grad in grads]
        for (slot, block), here, grad in zip(items, heres, grads):
            gain = gain_ref[0, pieces[slot][0]]
            grad_in, new = norm_back(part(slot, 0, here.start, here.stop), grad, gain)
            new_query[slot] = new_query[slot] + new
            span = slice(block * per, (block + 1) * per)
            result_ref[span, 3 * slot] = grad_in.reshape(per, rows, dim)

    for items in groups_of(count, blocks, KEY_GROUP):
        every = [
            (slot, slice(block * BLOCK, (block + 1) * BLOCK), min(tokens, (block + 1) * BLOCK + LONGEST))
            for slot, block in items
        ]
        grads = [
            dot(dscore_refs[slot, here, here.start : high], query_refs[slot, here.start : high])
            for slot, here, high in every
        ]
        value_grads = [
            dot(probs_refs[slot, here, here.start : high], part(slot, 3, here.start, high))
            for slot, here, high in every
        ]
        for (slot, block), here, grad, value_grad in zip(
            items, [here for _, here, _ in every], grads, value_grads
        ):
            gain = gain_ref[1, pieces[slot][0]]
            grad = (grad * scale).astype(BF16)
            grad_in, new = norm_back(part(slot, 1, here.start, here.stop), grad, gain)
            new_key[slot] = new_key[slot] + new
            span = slice(block * per, (block + 1) * per)
            result_ref[span, 3 * slot + 1] = grad_in.reshape(per, rows, dim)
            result_ref[span, 3 * slot + 2] = value_grad.astype(BF16).reshape(per, rows, dim)
    store = store_kinds(result_ref, out_ref, base, 0, 3 * count, store_sems.at[0, 0])
    for slot, (head, _) in enumerate(pieces):
        new_ref[0, head] = new_query[slot]
        new_ref[1, head] = new_key[slot]
    store.wait()


ANYWHERE = pl.BlockSpec(memory_space=pl.ANY)
IN_VMEM = pl.BlockSpec(memory_space=pltpu.VMEM)
VMEM_LIMIT = 40 * 1024 * 1024
KINDS_IN = {"f": 3, "b": 4}
KINDS_OUT = {"f": 1, "b": 3}


def places(pieces, kinds):
    found, at = {}, 0
    for piece in pieces:
        found[piece] = at
        at += kinds[piece[0]]
    return found, at


def pack_kernel(pieces, ranks, *refs):
    *in_refs, out_ref, held_ref, load_sems, store_sems = refs
    dim = out_ref.shape[-1]
    heads = held_ref.shape[2] // (ranks * dim)
    loads, at = [], 0
    for index, ref in enumerate(in_refs):
        kinds = ref.shape[0]
        loads.append(pltpu.make_async_copy(ref, held_ref.at[at : at + kinds], load_sems.at[index]))
        loads[-1].start()
        at += kinds
    spans, at, index = {}, 0, 0
    stores, slot = [], 0
    for number, (name, head) in enumerate(pieces):
        if name not in spans:
            spans[name] = at
            for _ in range(1 if name == "f" else 2):
                loads[index].wait()
                index += 1
            at += KINDS_IN[name]
        kinds = KINDS_IN[name]
        for rank in range(ranks):
            low = (rank * heads + head) * dim
            store = pltpu.make_async_copy(
                held_ref.at[spans[name] : spans[name] + kinds, :, low : low + dim],
                out_ref.at[rank, slot : slot + kinds],
                store_sems.at[number, rank],
            )
            store.start()
            stores.append(store)
        slot += kinds
    for store in stores:
        store.wait()


def pack(sources, pieces, ranks, dim):
    names = list(dict.fromkeys(name for name, _ in pieces))
    arrays = [array for name in names for array in sources[name]]
    rows, width = arrays[0].shape[1:]
    held = sum(array.shape[0] for array in arrays)
    kinds = places(pieces, KINDS_IN)[1]
    return pl.pallas_call(
        functools.partial(pack_kernel, pieces, ranks),
        in_specs=[ANYWHERE] * len(arrays),
        out_specs=ANYWHERE,
        out_shape=pltpu.HBM((ranks, kinds, rows, dim), arrays[0].dtype),
        scratch_shapes=[
            pltpu.VMEM((held, rows, width), arrays[0].dtype),
            pltpu.SemaphoreType.DMA((len(arrays),)),
            pltpu.SemaphoreType.DMA((len(pieces), ranks)),
        ],
        compiler_params=pltpu.CompilerParams(vmem_limit_bytes=VMEM_LIMIT),
        name="pack",
    )(*[pltpu.with_memory_space_constraint(array, pltpu.HBM) for array in arrays])


def unpack_kernel(count, in_ref, *refs):
    *out_refs, sems = refs
    ranks, _, _, dim = in_ref.shape
    copies, first = [], 0
    for number, out_ref in enumerate(out_refs):
        kinds = out_ref.shape[0]
        for head in range(count):
            for rank in range(ranks):
                low = (rank * count + head) * dim
                copies.append(
                    pltpu.make_async_copy(
                        in_ref.at[rank, first : first + kinds],
                        out_ref.at[:, :, low : low + dim],
                        sems.at[number, head, rank],
                    )
                )
            first += kinds
    for copy in copies:
        copy.start()
    for copy in copies:
        copy.wait()


def unpack(array, names, heads):
    ranks, _, rows, dim = array.shape
    return pl.pallas_call(
        functools.partial(unpack_kernel, heads),
        in_specs=[ANYWHERE],
        out_specs=[ANYWHERE] * len(names),
        out_shape=[
            pltpu.HBM((KINDS_OUT[name], rows, ranks * heads * dim), array.dtype) for name in names
        ],
        scratch_shapes=[pltpu.SemaphoreType.DMA((len(names), heads, ranks))],
        compiler_params=pltpu.CompilerParams(vmem_limit_bytes=VMEM_LIMIT),
        name="unpack",
    )(array)


def attend(name, group, pieces, gain, docs, kinds, base, out, settled):
    if settled:
        group = pltpu.with_memory_space_constraint(group, pltpu.HBM)
    ranks, _, rows, dim = group.shape
    tokens = ranks * rows
    count = len(pieces)
    row_major = pltpu.VMEM((count, tokens, dim), BF16)
    col_major = pltpu.VMEM((count, dim, tokens), BF16)
    square = pltpu.VMEM((count, tokens, tokens), BF16)
    kinds_in, kinds_out = KINDS_IN[name], KINDS_OUT[name] * count
    scratch = [
        pltpu.VMEM((count, ranks, kinds_in, rows, dim), BF16),
        pltpu.VMEM((ranks, kinds_out, rows, dim), BF16),
        pltpu.SemaphoreType.DMA((count,)),
        pltpu.SemaphoreType.DMA((count, 2)),
        row_major,
        row_major,
        col_major,
    ]
    out_shape = [pltpu.HBM((ranks, kinds, rows, dim), group.dtype)]
    if name == "b":
        scratch += [col_major, col_major, square, square]
        out_shape.append(jax.ShapeDtypeStruct(gain.shape, F32))
    dots = 2 if name == "f" else 6
    return pl.pallas_call(
        functools.partial(forward_kernel if name == "f" else backward_kernel, pieces, base),
        in_specs=[ANYWHERE, IN_VMEM, IN_VMEM] + [ANYWHERE] * len(out),
        out_specs=[ANYWHERE, IN_VMEM][: len(out_shape)],
        out_shape=out_shape,
        scratch_shapes=scratch,
        input_output_aliases={3: 0} if out else {},
        compiler_params=pltpu.CompilerParams(vmem_limit_bytes=VMEM_LIMIT),
        cost_estimate=pl.CostEstimate(
            flops=count * dots * tokens * tokens * dim,
            bytes_accessed=count * tokens * dim * 2 * (KINDS_IN[name] + KINDS_OUT[name]),
            transcendentals=count * tokens * tokens // 2,
        ),
        name="forward" if name == "f" else "backward",
    )(group, gain, docs, *out)


def exchange(value):
    return lax.all_to_all(value, "head", split_axis=0, concat_axis=0, tiled=True)


def after(value, earlier):
    return value if earlier is None else lax.optimization_barrier((value, earlier))[0]


def copy_kernel(in_ref, out_ref, sem):
    copy = pltpu.make_async_copy(in_ref, out_ref, sem)
    copy.start()
    copy.wait()


def into_hbm(array):
    return pl.pallas_call(
        copy_kernel,
        in_specs=[IN_VMEM],
        out_specs=ANYWHERE,
        out_shape=pltpu.HBM(array.shape, array.dtype),
        scratch_shapes=[pltpu.SemaphoreType.DMA(())],
        name="settle",
    )(array)


F0, F1, B0, B1 = ("f", 0), ("f", 1), ("b", 0), ("b", 1)
PLANS = (
    (((B0, B1, F0, F1),), (("b",), ("f",))),
    (((B0, B1), (F0, F1)), (("b", "f"),)),
)


def branch(plan, mirror, fwd_raw, bwd_raw, upstream, norm_gain, fwd_docs, bwd_docs, accum):
    ranks = lax.axis_size("head")
    pipe_count = lax.axis_size("pipe")
    pipe_at = lax.axis_index("pipe")
    heads, dim = norm_gain.shape[2] // ranks, norm_gain.shape[3]
    head_at = lax.axis_index("head") * heads
    sources = {"f": [fwd_raw], "b": [bwd_raw, upstream]}
    sections = {"f": pipe_at, "b": pipe_count - 1 - pipe_at}
    gains = {
        name: lax.dynamic_slice(norm_gain, (at, 0, head_at, 0), (1, 2, heads, dim)).reshape(
            2, heads, 1, dim
        )
        for name, at in sections.items()
    }
    docs = {"f": fwd_docs, "b": bwd_docs}
    ins, outs = plan
    latest, where = None, {}
    for pieces in ins:
        latest = exchange(after(pack(sources, pieces, ranks, dim), latest))
        for (name, head), first in places(pieces, KINDS_IN)[0].items():
            where.setdefault(name, (latest, []))[1].append((head, first))
    held, earlier = {}, None
    for names in outs:
        out, base = (), 0
        kinds = sum(KINDS_OUT[name] for name in names) * heads
        for name in names:
            group, pieces = where[name]
            results, *new = attend(
                name, after(group, earlier), tuple(pieces), gains[name], docs[name], kinds, base, out,
                len(ins) == 1 or group is not latest,
            )
            if new:
                up_local = accum[1] + new[0].reshape(accum[1].shape)
                mirrored = lax.ppermute(up_local, "pipe", mirror)
                total = lax.psum(accum[0] + mirrored, "dp")
            out, earlier = (results,), results
            base += KINDS_OUT[name] * heads
        latest = exchange(after(results, (latest, total) if held.get("b") is not None else latest))
        held.update(zip(names, unpack(latest, names, heads)))
    return held["b"], held["f"], into_hbm(total)


def body(fwd_qkv, bwd_qkv, bwd_grad_out, fwd_doc, bwd_doc, norm_gain, grad_acc):
    ranks = lax.axis_size("head")
    pipe_count = lax.axis_size("pipe")
    pipe_at = lax.axis_index("pipe")
    tokens = fwd_qkv.shape[2]
    width = fwd_qkv.shape[4]
    dim = norm_gain.shape[3]
    local_heads = norm_gain.shape[2] // ranks

    args = (
        fwd_qkv.reshape(tokens, 3, width).transpose(1, 0, 2),
        bwd_qkv.reshape(tokens, 3, width).transpose(1, 0, 2),
        bwd_grad_out.reshape(1, tokens, width),
        norm_gain,
        fwd_doc.reshape(-1, BLOCK),
        bwd_doc.reshape(-1, BLOCK),
        grad_acc.reshape(2, 2, local_heads, dim),
    )
    plans = [(at ^ (at >> 1)) & 1 for at in range(pipe_count)]
    mirrors = [
        [(at, pipe_count - 1 - at) for at in range(pipe_count) if plans[at] == plan]
        for plan in range(2)
    ]
    qkv_grad, fwd_out, total = lax.cond(
        (pipe_at ^ (pipe_at >> 1)) & 1 == 0,
        functools.partial(branch, PLANS[0], mirrors[0]),
        functools.partial(branch, PLANS[1], mirrors[1]),
        *args,
    )
    return (
        fwd_out.reshape(1, 1, tokens, width),
        qkv_grad.transpose(1, 0, 2).reshape(1, 1, tokens, 3, width),
        total.reshape(1, 2, local_heads, dim),
    )


def solution(mesh):
    in_specs = (
        P("dp", "pipe", "head", None, None),
        P("dp", "pipe", "head", None, None),
        P("dp", "pipe", "head", None),
        P("dp", "pipe", None),
        P("dp", "pipe", None),
        P(),
        P("dp", "pipe", None, None, "head", None),
    )
    out_specs = (
        P("dp", "pipe", "head", None),
        P("dp", "pipe", "head", None, None),
        P("pipe", None, "head", None),
    )
    return jax.shard_map(body, mesh=mesh, in_specs=in_specs, out_specs=out_specs, check_vma=False)
```

```python
import functools
import math

import jax
import jax.numpy as jnp
from jax import lax
from jax.experimental import pallas as pl
from jax.experimental.pallas import tpu as pltpu
from jax.sharding import PartitionSpec as P

EPS = 1e-06
LONGEST = 512
BLOCK = 256
NT = (((1,), (1,)), ((), ()))
NN = (((1,), (0,)), ((), ()))
F32 = jnp.float32
BF16 = jnp.bfloat16


def dot(left, right, dims=NN):
    return lax.dot_general(left, right, dims, preferred_element_type=F32)


def unit_of(raw):
    values = raw.astype(F32)
    recip = lax.rsqrt(jnp.mean(values * values, axis=-1, keepdims=True) + EPS)
    return values * recip, recip


def starts_of(docs):
    first = jnp.zeros(docs.shape, jnp.int32)
    for value in range(3):
        count = jnp.sum((docs == value).astype(jnp.int32))
        first = first + jnp.where(docs > value, count, 0)
    return first


def window(block):
    low = max(0, block * BLOCK - LONGEST)
    return low, (block + 1) * BLOCK


FORWARD_GROUP, BACKWARD_GROUP, KEY_GROUP = 4, 4, 4


def groups_of(count, blocks, size):
    items = [(slot, block) for block in range(blocks) for slot in range(count)]
    return [items[at : at + size] for at in range(0, len(items), size)]


def probs_of(scores, starts, spans, dim):
    factor = math.log2(math.e) / math.sqrt(dim)
    rows = lax.broadcasted_iota(jnp.int32, (BLOCK, BLOCK), 0)
    cols = lax.broadcasted_iota(jnp.int32, (BLOCK, BLOCK), 1)
    lists = []
    for score, start, (low, high) in zip(scores, starts, spans):
        pieces = []
        for at in range(low, high, BLOCK):
            allowed = rows >= start - at
            if at + BLOCK == high:
                allowed = allowed & (rows <= cols)
            pieces.append(jnp.where(allowed, score[at - low : at - low + BLOCK], -1e30))
        lists.append(pieces)
    peaks = [
        jnp.max(functools.reduce(jnp.maximum, pieces), axis=0, keepdims=True) for pieces in lists
    ]
    lists = [
        [jnp.exp2((piece - peak) * factor) for piece in pieces] for pieces, peak in zip(lists, peaks)
    ]
    shares = [
        1.0 / jnp.sum(functools.reduce(jnp.add, pieces), axis=0, keepdims=True) for pieces in lists
    ]
    return [[piece * share for piece in pieces] for pieces, share in zip(lists, shares)]


def flat(ref, kind):
    ranks, _, rows, dim = ref.shape
    return ref[:, kind].reshape(ranks * rows, dim)


def load_pieces(pieces, group_ref, raw_refs, sems):
    kinds = raw_refs.shape[2]
    loads = [
        pltpu.make_async_copy(group_ref.at[:, first : first + kinds], raw_refs.at[slot], sems.at[slot])
        for slot, (_, first) in enumerate(pieces)
    ]
    for load in loads:
        load.start()
    return loads


def store_kinds(result_ref, out_ref, base, first, count, sem):
    out_part = out_ref.at[:, base + first : base + first + count]
    store = pltpu.make_async_copy(result_ref.at[:, first : first + count], out_part, sem)
    store.start()
    return store


def forward_kernel(pieces, base, group_ref, gain_ref, doc_ref, *refs):
    (
        out_ref, raw_refs, result_ref, load_sems, store_sems, query_ref, key_ref, value_t_ref,
    ) = refs[-8:]
    loads = load_pieces(pieces, group_ref, raw_refs, load_sems)
    rows, dim = group_ref.shape[2:]
    starts = starts_of(doc_ref[...])
    per = BLOCK // rows
    for slot, (head, _) in enumerate(pieces):
        loads[slot].wait()
        raw_ref = raw_refs.at[slot]
        gain = gain_ref[:, head]
        query_ref[slot] = (unit_of(flat(raw_ref, 0))[0] * gain[0]).astype(BF16)
        key_ref[slot] = (unit_of(flat(raw_ref, 1))[0] * gain[1]).astype(BF16)
        value_t_ref[slot] = flat(raw_ref, 2).T
    for items in groups_of(len(pieces), query_ref.shape[1] // BLOCK, FORWARD_GROUP):
        spans = [window(block) for _, block in items]
        scores = [
            dot(key_ref[slot, low:high], query_ref[slot, block * BLOCK : high], NT)
            for (slot, block), (low, high) in zip(items, spans)
        ]
        probs = probs_of(scores, [starts[block : block + 1] for _, block in items], spans, dim)
        probs = [jnp.concatenate([piece.astype(BF16) for piece in every], axis=0) for every in probs]
        results = [
            dot(value_t_ref[slot, :, low:high], prob)
            for (slot, _), (low, high), prob in zip(items, spans, probs)
        ]
        for (slot, block), result in zip(items, results):
            result = result.T.astype(BF16).reshape(per, rows, dim)
            result_ref[block * per : (block + 1) * per, slot] = result
    store_kinds(result_ref, out_ref, base, 0, len(pieces), store_sems.at[0, 0]).wait()


def norm_back(raw, grad, gain):
    unit, recip = unit_of(raw)
    normed = grad.astype(F32)
    scaled = normed * gain
    grad_in = recip * (scaled - unit * jnp.mean(scaled * unit, axis=-1, keepdims=True))
    return grad_in.astype(BF16), jnp.sum(normed * unit, axis=0, keepdims=True)


def backward_kernel(pieces, base, group_ref, gain_ref, doc_ref, *refs):
    (
        out_ref, new_ref, raw_refs, result_ref, load_sems, store_sems,
        query_refs, key_refs, key_t_refs, value_t_refs, up_t_refs, probs_refs, dscore_refs,
    ) = refs[-13:]
    loads = load_pieces(pieces, group_ref, raw_refs, load_sems)
    rows, dim = group_ref.shape[2:]
    tokens = query_refs.shape[1]
    scale = 1.0 / math.sqrt(dim)
    starts = starts_of(doc_ref[...])
    per = BLOCK // rows
    blocks = tokens // BLOCK
    count = len(pieces)

    def part(slot, kind, low, high):
        return raw_refs[slot, low // rows : high // rows, kind].reshape(high - low, dim)

    for slot, (head, _) in enumerate(pieces):
        loads[slot].wait()
        gain = gain_ref[:, head]
        query_refs[slot] = (unit_of(part(slot, 0, 0, tokens))[0] * gain[0]).astype(BF16)
        key = (unit_of(part(slot, 1, 0, tokens))[0] * gain[1]).astype(BF16)
        key_refs[slot] = key
        key_t_refs[slot] = key.T
        value_t_refs[slot] = part(slot, 2, 0, tokens).T
        up_t_refs[slot] = part(slot, 3, 0, tokens).T
    new_query = [jnp.zeros((1, dim), F32)] * count
    new_key = [jnp.zeros((1, dim), F32)] * count
    for items in groups_of(count, blocks, BACKWARD_GROUP):
        spans = [window(block) for _, block in items]
        heres = [slice(block * BLOCK, (block + 1) * BLOCK) for _, block in items]
        every = [(slot, low, high, here) for (slot, _), (low, high), here in zip(items, spans, heres)]
        scores = [
            dot(key_refs[slot, low:high], query_refs[slot, here], NT) for slot, low, high, here in every
        ]
        dprobs = [
            dot(part(slot, 2, low, high), part(slot, 3, here.start, here.stop), NT)
            for slot, low, high, here in every
        ]
        probs = probs_of(scores, [starts[block : block + 1] for _, block in items], spans, dim)
        rounded = [jnp.concatenate([piece.astype(BF16) for piece in some], axis=0) for some in probs]
        results = [
            dot(value_t_refs[slot, :, low:high], some)
            for (slot, low, high, _), some in zip(every, rounded)
        ]
        for (slot, low, high, here), some in zip(every, rounded):
            probs_refs[slot, low:high, here] = some
        dsums = [
            jnp.sum(up_t_refs[slot, :, here].astype(F32) * result, axis=0, keepdims=True)
            for (slot, _, _, here), result in zip(every, results)
        ]
        dscores = [
            jnp.concatenate(
                [
                    (piece * (dprob[at * BLOCK : (at + 1) * BLOCK] - dsum)).astype(BF16)
                    for at, piece in enumerate(some)
                ],
                axis=0,
            )
            for some, dprob, dsum in zip(probs, dprobs, dsums)
        ]
        grads = [
            dot(key_t_refs[slot, :, low:high], dscore) * scale
            for (slot, low, high, _), dscore in zip(every, dscores)
        ]
        for (slot, low, high, here), dscore in zip(every, dscores):
            dscore_refs[slot, low:high, here] = dscore
        grads = [grad.T.astype(BF16) for grad in grads]
        for (slot, block), here, grad in zip(items, heres, grads):
            gain = gain_ref[0, pieces[slot][0]]
            grad_in, new = norm_back(part(slot, 0, here.start, here.stop), grad, gain)
            new_query[slot] = new_query[slot] + new
            span = slice(block * per, (block + 1) * per)
            result_ref[span, 3 * slot] = grad_in.reshape(per, rows, dim)

    for items in groups_of(count, blocks, KEY_GROUP):
        every = [
            (slot, slice(block * BLOCK, (block + 1) * BLOCK), min(tokens, (block + 1) * BLOCK + LONGEST))
            for slot, block in items
        ]
        grads = [
            dot(dscore_refs[slot, here, here.start : high], query_refs[slot, here.start : high])
            for slot, here, high in every
        ]
        value_grads = [
            dot(probs_refs[slot, here, here.start : high], part(slot, 3, here.start, high))
            for slot, here, high in every
        ]
        for (slot, block), here, grad, value_grad in zip(
            items, [here for _, here, _ in every], grads, value_grads
        ):
            gain = gain_ref[1, pieces[slot][0]]
            grad = (grad * scale).astype(BF16)
            grad_in, new = norm_back(part(slot, 1, here.start, here.stop), grad, gain)
            new_key[slot] = new_key[slot] + new
            span = slice(block * per, (block + 1) * per)
            result_ref[span, 3 * slot + 1] = grad_in.reshape(per, rows, dim)
            result_ref[span, 3 * slot + 2] = value_grad.astype(BF16).reshape(per, rows, dim)
    store = store_kinds(result_ref, out_ref, base, 0, 3 * count, store_sems.at[0, 0])
    for slot, (head, _) in enumerate(pieces):
        new_ref[0, head] = new_query[slot]
        new_ref[1, head] = new_key[slot]
    store.wait()


ANYWHERE = pl.BlockSpec(memory_space=pl.ANY)
IN_VMEM = pl.BlockSpec(memory_space=pltpu.VMEM)
VMEM_LIMIT = 40 * 1024 * 1024
KINDS_IN = {"f": 3, "b": 4}
KINDS_OUT = {"f": 1, "b": 3}


def places(pieces, kinds):
    found, at = {}, 0
    for piece in pieces:
        found[piece] = at
        at += kinds[piece[0]]
    return found, at


def pack_kernel(pieces, ranks, *refs):
    *in_refs, out_ref, held_ref, load_sems, store_sems = refs
    dim = out_ref.shape[-1]
    heads = held_ref.shape[2] // (ranks * dim)
    loads, at = [], 0
    for index, ref in enumerate(in_refs):
        kinds = ref.shape[0]
        loads.append(pltpu.make_async_copy(ref, held_ref.at[at : at + kinds], load_sems.at[index]))
        loads[-1].start()
        at += kinds
    spans, at, index = {}, 0, 0
    stores, slot = [], 0
    for number, (name, head) in enumerate(pieces):
        if name not in spans:
            spans[name] = at
            for _ in range(1 if name == "f" else 2):
                loads[index].wait()
                index += 1
            at += KINDS_IN[name]
        kinds = KINDS_IN[name]
        for rank in range(ranks):
            low = (rank * heads + head) * dim
            store = pltpu.make_async_copy(
                held_ref.at[spans[name] : spans[name] + kinds, :, low : low + dim],
                out_ref.at[rank, slot : slot + kinds],
                store_sems.at[number, rank],
            )
            store.start()
            stores.append(store)
        slot += kinds
    for store in stores:
        store.wait()


def pack(sources, pieces, ranks, dim):
    names = list(dict.fromkeys(name for name, _ in pieces))
    arrays = [array for name in names for array in sources[name]]
    rows, width = arrays[0].shape[1:]
    held = sum(array.shape[0] for array in arrays)
    kinds = places(pieces, KINDS_IN)[1]
    return pl.pallas_call(
        functools.partial(pack_kernel, pieces, ranks),
        in_specs=[ANYWHERE] * len(arrays),
        out_specs=ANYWHERE,
        out_shape=pltpu.HBM((ranks, kinds, rows, dim), arrays[0].dtype),
        scratch_shapes=[
            pltpu.VMEM((held, rows, width), arrays[0].dtype),
            pltpu.SemaphoreType.DMA((len(arrays),)),
            pltpu.SemaphoreType.DMA((len(pieces), ranks)),
        ],
        compiler_params=pltpu.CompilerParams(vmem_limit_bytes=VMEM_LIMIT),
        name="pack",
    )(*[pltpu.with_memory_space_constraint(array, pltpu.HBM) for array in arrays])


def unpack_kernel(count, in_ref, *refs):
    *out_refs, sems = refs
    ranks, _, _, dim = in_ref.shape
    copies, first = [], 0
    for number, out_ref in enumerate(out_refs):
        kinds = out_ref.shape[0]
        for head in range(count):
            for rank in range(ranks):
                low = (rank * count + head) * dim
                copies.append(
                    pltpu.make_async_copy(
                        in_ref.at[rank, first : first + kinds],
                        out_ref.at[:, :, low : low + dim],
                        sems.at[number, head, rank],
                    )
                )
            first += kinds
    for copy in copies:
        copy.start()
    for copy in copies:
        copy.wait()


def unpack(array, names, heads):
    ranks, _, rows, dim = array.shape
    return pl.pallas_call(
        functools.partial(unpack_kernel, heads),
        in_specs=[ANYWHERE],
        out_specs=[ANYWHERE] * len(names),
        out_shape=[
            pltpu.HBM((KINDS_OUT[name], rows, ranks * heads * dim), array.dtype) for name in names
        ],
        scratch_shapes=[pltpu.SemaphoreType.DMA((len(names), heads, ranks))],
        compiler_params=pltpu.CompilerParams(vmem_limit_bytes=VMEM_LIMIT),
        name="unpack",
    )(array)


def attend(name, group, pieces, gain, docs, kinds, base, out, settled):
    if settled:
        group = pltpu.with_memory_space_constraint(group, pltpu.HBM)
    ranks, _, rows, dim = group.shape
    tokens = ranks * rows
    count = len(pieces)
    row_major = pltpu.VMEM((count, tokens, dim), BF16)
    col_major = pltpu.VMEM((count, dim, tokens), BF16)
    square = pltpu.VMEM((count, tokens, tokens), BF16)
    kinds_in, kinds_out = KINDS_IN[name], KINDS_OUT[name] * count
    scratch = [
        pltpu.VMEM((count, ranks, kinds_in, rows, dim), BF16),
        pltpu.VMEM((ranks, kinds_out, rows, dim), BF16),
        pltpu.SemaphoreType.DMA((count,)),
        pltpu.SemaphoreType.DMA((count, 2)),
        row_major,
        row_major,
        col_major,
    ]
    out_shape = [pltpu.HBM((ranks, kinds, rows, dim), group.dtype)]
    if name == "b":
        scratch += [col_major, col_major, square, square]
        out_shape.append(jax.ShapeDtypeStruct(gain.shape, F32))
    dots = 2 if name == "f" else 6
    return pl.pallas_call(
        functools.partial(forward_kernel if name == "f" else backward_kernel, pieces, base),
        in_specs=[ANYWHERE, IN_VMEM, IN_VMEM] + [ANYWHERE] * len(out),
        out_specs=[ANYWHERE, IN_VMEM][: len(out_shape)],
        out_shape=out_shape,
        scratch_shapes=scratch,
        input_output_aliases={3: 0} if out else {},
        compiler_params=pltpu.CompilerParams(vmem_limit_bytes=VMEM_LIMIT),
        cost_estimate=pl.CostEstimate(
            flops=count * dots * tokens * tokens * dim,
            bytes_accessed=count * tokens * dim * 2 * (KINDS_IN[name] + KINDS_OUT[name]),
            transcendentals=count * tokens * tokens // 2,
        ),
        name="forward" if name == "f" else "backward",
    )(group, gain, docs, *out)


def exchange(value):
    return lax.all_to_all(value, "head", split_axis=0, concat_axis=0, tiled=True)


def after(value, earlier):
    return value if earlier is None else lax.optimization_barrier((value, earlier))[0]


def copy_kernel(in_ref, out_ref, sem):
    copy = pltpu.make_async_copy(in_ref, out_ref, sem)
    copy.start()
    copy.wait()


def into_hbm(array):
    return pl.pallas_call(
        copy_kernel,
        in_specs=[IN_VMEM],
        out_specs=ANYWHERE,
        out_shape=pltpu.HBM(array.shape, array.dtype),
        scratch_shapes=[pltpu.SemaphoreType.DMA(())],
        name="settle",
    )(array)


F0, F1, B0, B1 = ("f", 0), ("f", 1), ("b", 0), ("b", 1)
PLANS = (
    (((B0, B1, F0, F1),), (("b",), ("f",))),
    (((B0, B1), (F0, F1)), (("b", "f"),)),
)


def branch(plan, mirror, fwd_raw, bwd_raw, upstream, norm_gain, fwd_docs, bwd_docs, accum):
    ranks = lax.axis_size("head")
    pipe_count = lax.axis_size("pipe")
    pipe_at = lax.axis_index("pipe")
    heads, dim = norm_gain.shape[2] // ranks, norm_gain.shape[3]
    head_at = lax.axis_index("head") * heads
    sources = {"f": [fwd_raw], "b": [bwd_raw, upstream]}
    sections = {"f": pipe_at, "b": pipe_count - 1 - pipe_at}
    gains = {
        name: lax.dynamic_slice(norm_gain, (at, 0, head_at, 0), (1, 2, heads, dim)).reshape(
            2, heads, 1, dim
        )
        for name, at in sections.items()
    }
    docs = {"f": fwd_docs, "b": bwd_docs}
    ins, outs = plan
    latest, where = None, {}
    for pieces in ins:
        latest = exchange(after(pack(sources, pieces, ranks, dim), latest))
        for (name, head), first in places(pieces, KINDS_IN)[0].items():
            where.setdefault(name, (latest, []))[1].append((head, first))
    held, earlier = {}, None
    for names in outs:
        out, base = (), 0
        kinds = sum(KINDS_OUT[name] for name in names) * heads
        for name in names:
            group, pieces = where[name]
            results, *new = attend(
                name, after(group, earlier), tuple(pieces), gains[name], docs[name], kinds, base, out,
                len(ins) == 1 or group is not latest,
            )
            if new:
                up_local = accum[1] + new[0].reshape(accum[1].shape)
                mirrored = lax.ppermute(up_local, "pipe", mirror)
                total = lax.psum(accum[0] + mirrored, "dp")
            out, earlier = (results,), results
            base += KINDS_OUT[name] * heads
        latest = exchange(after(results, (latest, total) if held.get("b") is not None else latest))
        held.update(zip(names, unpack(latest, names, heads)))
    return held["b"], held["f"], into_hbm(total)


def body(fwd_qkv, bwd_qkv, bwd_grad_out, fwd_doc, bwd_doc, norm_gain, grad_acc):
    ranks = lax.axis_size("head")
    pipe_count = lax.axis_size("pipe")
    pipe_at = lax.axis_index("pipe")
    tokens = fwd_qkv.shape[2]
    width = fwd_qkv.shape[4]
    dim = norm_gain.shape[3]
    local_heads = norm_gain.shape[2] // ranks

    args = (
        fwd_qkv.reshape(tokens, 3, width).transpose(1, 0, 2),
        bwd_qkv.reshape(tokens, 3, width).transpose(1, 0, 2),
        bwd_grad_out.reshape(1, tokens, width),
        norm_gain,
        fwd_doc.reshape(-1, BLOCK),
        bwd_doc.reshape(-1, BLOCK),
        grad_acc.reshape(2, 2, local_heads, dim),
    )
    plans = [(at ^ (at >> 1)) & 1 for at in range(pipe_count)]
    mirrors = [
        [(at, pipe_count - 1 - at) for at in range(pipe_count) if plans[at] == plan]
        for plan in range(2)
    ]
    qkv_grad, fwd_out, total = lax.cond(
        (pipe_at ^ (pipe_at >> 1)) & 1 == 0,
        functools.partial(branch, PLANS[0], mirrors[0]),
        functools.partial(branch, PLANS[1], mirrors[1]),
        *args,
    )
    return (
        fwd_out.reshape(1, 1, tokens, width),
        qkv_grad.transpose(1, 0, 2).reshape(1, 1, tokens, 3, width),
        total.reshape(1, 2, local_heads, dim),
    )


def solution(mesh):
    in_specs = (
        P("dp", "pipe", "head", None, None),
        P("dp", "pipe", "head", None, None),
        P("dp", "pipe", "head", None),
        P("dp", "pipe", None),
        P("dp", "pipe", None),
        P(),
        P("dp", "pipe", None, None, "head", None),
    )
    out_specs = (
        P("dp", "pipe", "head", None),
        P("dp", "pipe", "head", None, None),
        P("pipe", None, "head", None),
    )
    return jax.shard_map(body, mesh=mesh, in_specs=in_specs, out_specs=out_specs, check_vma=False)
```

```python
import functools
import math

import jax
import jax.numpy as jnp
from jax import lax
from jax.experimental import pallas as pl
from jax.experimental.pallas import tpu as pltpu
from jax.sharding import PartitionSpec as P

EPS = 1e-06
LONGEST = 512
BLOCK = 256
LANES = 128
NT = (((1,), (1,)), ((), ()))
NN = (((1,), (0,)), ((), ()))
F32 = jnp.float32
BF16 = jnp.bfloat16


def dot(left, right, dims=NN):
    return lax.dot_general(left, right, dims, preferred_element_type=F32)


def unit_of(raw):
    values = raw.astype(F32)
    recip = lax.rsqrt(jnp.mean(values * values, axis=-1, keepdims=True) + EPS)
    return values * recip, recip


def starts_of(docs):
    first = jnp.zeros(docs.shape, jnp.int32)
    for value in range(3):
        count = jnp.sum((docs == value).astype(jnp.int32))
        first = first + jnp.where(docs > value, count, 0)
    return first


def starts_at(starts, block):
    per = BLOCK // LANES
    return jnp.concatenate([starts[at : at + 1] for at in range(block * per, (block + 1) * per)], axis=1)


def window(block):
    low = max(0, block * BLOCK - LONGEST)
    return low, (block + 1) * BLOCK


FORWARD_GROUP, BACKWARD_GROUP, KEY_GROUP = 4, 4, 4


def groups_of(count, blocks, size):
    items = [(slot, block) for block in range(blocks) for slot in range(count)]
    return [items[at : at + size] for at in range(0, len(items), size)]


def probs_of(scores, starts, spans, dim):
    factor = math.log2(math.e) / math.sqrt(dim)
    rows = lax.broadcasted_iota(jnp.int32, (BLOCK, BLOCK), 0)
    cols = lax.broadcasted_iota(jnp.int32, (BLOCK, BLOCK), 1)
    lists = []
    for score, start, (low, high) in zip(scores, starts, spans):
        pieces = []
        for at in range(low, high, BLOCK):
            allowed = rows >= start - at
            if at + BLOCK == high:
                allowed = allowed & (rows <= cols)
            pieces.append(jnp.where(allowed, score[at - low : at - low + BLOCK], -1e30))
        lists.append(pieces)
    peaks = [
        jnp.max(functools.reduce(jnp.maximum, pieces), axis=0, keepdims=True) for pieces in lists
    ]
    lists = [
        [jnp.exp2((piece - peak) * factor) for piece in pieces] for pieces, peak in zip(lists, peaks)
    ]
    shares = [
        1.0 / jnp.sum(functools.reduce(jnp.add, pieces), axis=0, keepdims=True) for pieces in lists
    ]
    return [[piece * share for piece in pieces] for pieces, share in zip(lists, shares)]


def flat(ref, kind):
    ranks, _, rows, dim = ref.shape
    return ref[:, kind].reshape(ranks * rows, dim)


def load_pieces(pieces, group_ref, raw_refs, sems):
    kinds = raw_refs.shape[2]
    loads = [
        pltpu.make_async_copy(group_ref.at[:, first : first + kinds], raw_refs.at[slot], sems.at[slot])
        for slot, (_, first) in enumerate(pieces)
    ]
    for load in loads:
        load.start()
    return loads


def store_kinds(result_ref, out_ref, base, first, count, sem):
    out_part = out_ref.at[:, base + first : base + first + count]
    store = pltpu.make_async_copy(result_ref.at[:, first : first + count], out_part, sem)
    store.start()
    return store


def forward_kernel(pieces, base, group_ref, gain_ref, doc_ref, *refs):
    (
        out_ref, raw_refs, result_ref, load_sems, store_sems, query_ref, key_ref, value_t_ref,
    ) = refs[-8:]
    loads = load_pieces(pieces, group_ref, raw_refs, load_sems)
    rows, dim = group_ref.shape[2:]
    starts = starts_of(doc_ref[...])
    per = BLOCK // rows
    for slot, (head, _) in enumerate(pieces):
        loads[slot].wait()
        raw_ref = raw_refs.at[slot]
        gain = gain_ref[:, head]
        query_ref[slot] = (unit_of(flat(raw_ref, 0))[0] * gain[0]).astype(BF16)
        key_ref[slot] = (unit_of(flat(raw_ref, 1))[0] * gain[1]).astype(BF16)
        value_t_ref[slot] = flat(raw_ref, 2).T
    for items in groups_of(len(pieces), query_ref.shape[1] // BLOCK, FORWARD_GROUP):
        spans = [window(block) for _, block in items]
        scores = [
            dot(key_ref[slot, low:high], query_ref[slot, block * BLOCK : high], NT)
            for (slot, block), (low, high) in zip(items, spans)
        ]
        probs = probs_of(scores, [starts_at(starts, block) for _, block in items], spans, dim)
        probs = [jnp.concatenate([piece.astype(BF16) for piece in every], axis=0) for every in probs]
        results = [
            dot(value_t_ref[slot, :, low:high], prob)
            for (slot, _), (low, high), prob in zip(items, spans, probs)
        ]
        for (slot, block), result in zip(items, results):
            result = result.T.astype(BF16).reshape(per, rows, dim)
            result_ref[block * per : (block + 1) * per, slot] = result
    store_kinds(result_ref, out_ref, base, 0, len(pieces), store_sems.at[0, 0]).wait()


def norm_back(raw, grad, gain):
    unit, recip = unit_of(raw)
    normed = grad.astype(F32)
    scaled = normed * gain
    grad_in = recip * (scaled - unit * jnp.mean(scaled * unit, axis=-1, keepdims=True))
    return grad_in.astype(BF16), jnp.sum(normed * unit, axis=0, keepdims=True)


def backward_kernel(pieces, base, group_ref, gain_ref, doc_ref, *refs):
    (
        out_ref, new_ref, raw_refs, result_ref, load_sems, store_sems,
        query_refs, key_refs, key_t_refs, value_t_refs, up_t_refs, probs_refs, dscore_refs,
    ) = refs[-13:]
    loads = load_pieces(pieces, group_ref, raw_refs, load_sems)
    rows, dim = group_ref.shape[2:]
    tokens = query_refs.shape[1]
    scale = 1.0 / math.sqrt(dim)
    starts = starts_of(doc_ref[...])
    per = BLOCK // rows
    blocks = tokens // BLOCK
    count = len(pieces)

    def part(slot, kind, low, high):
        return raw_refs[slot, low // rows : high // rows, kind].reshape(high - low, dim)

    for slot, (head, _) in enumerate(pieces):
        loads[slot].wait()
        gain = gain_ref[:, head]
        query_refs[slot] = (unit_of(part(slot, 0, 0, tokens))[0] * gain[0]).astype(BF16)
        key = (unit_of(part(slot, 1, 0, tokens))[0] * gain[1]).astype(BF16)
        key_refs[slot] = key
        key_t_refs[slot] = key.T
        value_t_refs[slot] = part(slot, 2, 0, tokens).T
        up_t_refs[slot] = part(slot, 3, 0, tokens).T
    new_query = [jnp.zeros((1, dim), F32)] * count
    new_key = [jnp.zeros((1, dim), F32)] * count
    for items in groups_of(count, blocks, BACKWARD_GROUP):
        spans = [window(block) for _, block in items]
        heres = [slice(block * BLOCK, (block + 1) * BLOCK) for _, block in items]
        every = [(slot, low, high, here) for (slot, _), (low, high), here in zip(items, spans, heres)]
        scores = [
            dot(key_refs[slot, low:high], query_refs[slot, here], NT) for slot, low, high, here in every
        ]
        dprobs = [
            dot(part(slot, 2, low, high), part(slot, 3, here.start, here.stop), NT)
            for slot, low, high, here in every
        ]
        probs = probs_of(scores, [starts_at(starts, block) for _, block in items], spans, dim)
        rounded = [jnp.concatenate([piece.astype(BF16) for piece in some], axis=0) for some in probs]
        results = [
            dot(value_t_refs[slot, :, low:high], some)
            for (slot, low, high, _), some in zip(every, rounded)
        ]
        for (slot, low, high, here), some in zip(every, rounded):
            probs_refs[slot, low:high, here] = some
        dsums = [
            jnp.sum(up_t_refs[slot, :, here].astype(F32) * result, axis=0, keepdims=True)
            for (slot, _, _, here), result in zip(every, results)
        ]
        dscores = [
            jnp.concatenate(
                [
                    (piece * (dprob[at * BLOCK : (at + 1) * BLOCK] - dsum)).astype(BF16)
                    for at, piece in enumerate(some)
                ],
                axis=0,
            )
            for some, dprob, dsum in zip(probs, dprobs, dsums)
        ]
        grads = [
            dot(key_t_refs[slot, :, low:high], dscore) * scale
            for (slot, low, high, _), dscore in zip(every, dscores)
        ]
        for (slot, low, high, here), dscore in zip(every, dscores):
            dscore_refs[slot, low:high, here] = dscore
        grads = [grad.T.astype(BF16) for grad in grads]
        for (slot, block), here, grad in zip(items, heres, grads):
            gain = gain_ref[0, pieces[slot][0]]
            grad_in, new = norm_back(part(slot, 0, here.start, here.stop), grad, gain)
            new_query[slot] = new_query[slot] + new
            span = slice(block * per, (block + 1) * per)
            result_ref[span, 3 * slot] = grad_in.reshape(per, rows, dim)

    for items in groups_of(count, blocks, KEY_GROUP):
        every = [
            (slot, slice(block * BLOCK, (block + 1) * BLOCK), min(tokens, (block + 1) * BLOCK + LONGEST))
            for slot, block in items
        ]
        grads = [
            dot(dscore_refs[slot, here, here.start : high], query_refs[slot, here.start : high])
            for slot, here, high in every
        ]
        value_grads = [
            dot(probs_refs[slot, here, here.start : high], part(slot, 3, here.start, high))
            for slot, here, high in every
        ]
        for (slot, block), here, grad, value_grad in zip(
            items, [here for _, here, _ in every], grads, value_grads
        ):
            gain = gain_ref[1, pieces[slot][0]]
            grad = (grad * scale).astype(BF16)
            grad_in, new = norm_back(part(slot, 1, here.start, here.stop), grad, gain)
            new_key[slot] = new_key[slot] + new
            span = slice(block * per, (block + 1) * per)
            result_ref[span, 3 * slot + 1] = grad_in.reshape(per, rows, dim)
            result_ref[span, 3 * slot + 2] = value_grad.astype(BF16).reshape(per, rows, dim)
    store = store_kinds(result_ref, out_ref, base, 0, 3 * count, store_sems.at[0, 0])
    for slot, (head, _) in enumerate(pieces):
        new_ref[0, head] = new_query[slot]
        new_ref[1, head] = new_key[slot]
    store.wait()


ANYWHERE = pl.BlockSpec(memory_space=pl.ANY)
IN_VMEM = pl.BlockSpec(memory_space=pltpu.VMEM)
VMEM_LIMIT = 40 * 1024 * 1024
KINDS_IN = {"f": 3, "b": 4}
KINDS_OUT = {"f": 1, "b": 3}


def places(pieces, kinds):
    found, at = {}, 0
    for piece in pieces:
        found[piece] = at
        at += kinds[piece[0]]
    return found, at


def pack_kernel(pieces, ranks, *refs):
    *in_refs, out_ref, held_ref, load_sems, store_sems = refs
    dim = out_ref.shape[-1]
    heads = held_ref.shape[2] // (ranks * dim)
    loads, at = [], 0
    for index, ref in enumerate(in_refs):
        kinds = ref.shape[0]
        loads.append(pltpu.make_async_copy(ref, held_ref.at[at : at + kinds], load_sems.at[index]))
        loads[-1].start()
        at += kinds
    spans, at, index = {}, 0, 0
    stores, slot = [], 0
    for number, (name, head) in enumerate(pieces):
        if name not in spans:
            spans[name] = at
            for _ in range(1 if name == "f" else 2):
                loads[index].wait()
                index += 1
            at += KINDS_IN[name]
        kinds = KINDS_IN[name]
        for rank in range(ranks):
            low = (rank * heads + head) * dim
            store = pltpu.make_async_copy(
                held_ref.at[spans[name] : spans[name] + kinds, :, low : low + dim],
                out_ref.at[rank, slot : slot + kinds],
                store_sems.at[number, rank],
            )
            store.start()
            stores.append(store)
        slot += kinds
    for store in stores:
        store.wait()


def pack(sources, pieces, ranks, dim):
    names = list(dict.fromkeys(name for name, _ in pieces))
    arrays = [array for name in names for array in sources[name]]
    rows, width = arrays[0].shape[1:]
    held = sum(array.shape[0] for array in arrays)
    kinds = places(pieces, KINDS_IN)[1]
    return pl.pallas_call(
        functools.partial(pack_kernel, pieces, ranks),
        in_specs=[ANYWHERE] * len(arrays),
        out_specs=ANYWHERE,
        out_shape=pltpu.HBM((ranks, kinds, rows, dim), arrays[0].dtype),
        scratch_shapes=[
            pltpu.VMEM((held, rows, width), arrays[0].dtype),
            pltpu.SemaphoreType.DMA((len(arrays),)),
            pltpu.SemaphoreType.DMA((len(pieces), ranks)),
        ],
        compiler_params=pltpu.CompilerParams(vmem_limit_bytes=VMEM_LIMIT),
        name="pack",
    )(*[pltpu.with_memory_space_constraint(array, pltpu.HBM) for array in arrays])


def unpack_kernel(count, in_ref, *refs):
    *out_refs, sems = refs
    ranks, _, _, dim = in_ref.shape
    copies, first = [], 0
    for number, out_ref in enumerate(out_refs):
        kinds = out_ref.shape[0]
        for head in range(count):
            for rank in range(ranks):
                low = (rank * count + head) * dim
                copies.append(
                    pltpu.make_async_copy(
                        in_ref.at[rank, first : first + kinds],
                        out_ref.at[:, :, low : low + dim],
                        sems.at[number, head, rank],
                    )
                )
            first += kinds
    for copy in copies:
        copy.start()
    for copy in copies:
        copy.wait()


def unpack(array, names, heads):
    ranks, _, rows, dim = array.shape
    return pl.pallas_call(
        functools.partial(unpack_kernel, heads),
        in_specs=[ANYWHERE],
        out_specs=[ANYWHERE] * len(names),
        out_shape=[
            pltpu.HBM((KINDS_OUT[name], rows, ranks * heads * dim), array.dtype) for name in names
        ],
        scratch_shapes=[pltpu.SemaphoreType.DMA((len(names), heads, ranks))],
        compiler_params=pltpu.CompilerParams(vmem_limit_bytes=VMEM_LIMIT),
        name="unpack",
    )(array)


def attend(name, group, pieces, gain, docs, kinds, base, out, settled):
    if settled:
        group = pltpu.with_memory_space_constraint(group, pltpu.HBM)
    ranks, _, rows, dim = group.shape
    tokens = ranks * rows
    count = len(pieces)
    row_major = pltpu.VMEM((count, tokens, dim), BF16)
    col_major = pltpu.VMEM((count, dim, tokens), BF16)
    square = pltpu.VMEM((count, tokens, tokens), BF16)
    kinds_in, kinds_out = KINDS_IN[name], KINDS_OUT[name] * count
    scratch = [
        pltpu.VMEM((count, ranks, kinds_in, rows, dim), BF16),
        pltpu.VMEM((ranks, kinds_out, rows, dim), BF16),
        pltpu.SemaphoreType.DMA((count,)),
        pltpu.SemaphoreType.DMA((count, 2)),
        row_major,
        row_major,
        col_major,
    ]
    out_shape = [pltpu.HBM((ranks, kinds, rows, dim), group.dtype)]
    if name == "b":
        scratch += [col_major, col_major, square, square]
        out_shape.append(jax.ShapeDtypeStruct(gain.shape, F32))
    dots = 2 if name == "f" else 6
    return pl.pallas_call(
        functools.partial(forward_kernel if name == "f" else backward_kernel, pieces, base),
        in_specs=[ANYWHERE, IN_VMEM, IN_VMEM] + [ANYWHERE] * len(out),
        out_specs=[ANYWHERE, IN_VMEM][: len(out_shape)],
        out_shape=out_shape,
        scratch_shapes=scratch,
        input_output_aliases={3: 0} if out else {},
        compiler_params=pltpu.CompilerParams(vmem_limit_bytes=VMEM_LIMIT),
        cost_estimate=pl.CostEstimate(
            flops=count * dots * tokens * tokens * dim,
            bytes_accessed=count * tokens * dim * 2 * (KINDS_IN[name] + KINDS_OUT[name]),
            transcendentals=count * tokens * tokens // 2,
        ),
        name="forward" if name == "f" else "backward",
    )(group, gain, docs, *out)


def exchange(value):
    return lax.all_to_all(value, "head", split_axis=0, concat_axis=0, tiled=True)


def after(value, earlier):
    return value if earlier is None else lax.optimization_barrier((value, earlier))[0]


def copy_kernel(in_ref, out_ref, sem):
    copy = pltpu.make_async_copy(in_ref, out_ref, sem)
    copy.start()
    copy.wait()


def into_hbm(array):
    return pl.pallas_call(
        copy_kernel,
        in_specs=[IN_VMEM],
        out_specs=ANYWHERE,
        out_shape=pltpu.HBM(array.shape, array.dtype),
        scratch_shapes=[pltpu.SemaphoreType.DMA(())],
        name="settle",
    )(array)


F0, F1, B0, B1 = ("f", 0), ("f", 1), ("b", 0), ("b", 1)
PLANS = (
    (((B0, B1, F0, F1),), (("b",), ("f",))),
    (((B0, B1), (F0, F1)), (("b", "f"),)),
)


def branch(plan, mirror, fwd_raw, bwd_raw, upstream, norm_gain, fwd_docs, bwd_docs, accum):
    ranks = lax.axis_size("head")
    pipe_count = lax.axis_size("pipe")
    pipe_at = lax.axis_index("pipe")
    heads, dim = norm_gain.shape[2] // ranks, norm_gain.shape[3]
    head_at = lax.axis_index("head") * heads
    sources = {"f": [fwd_raw], "b": [bwd_raw, upstream]}
    sections = {"f": pipe_at, "b": pipe_count - 1 - pipe_at}
    gains = {
        name: lax.dynamic_slice(norm_gain, (at, 0, head_at, 0), (1, 2, heads, dim)).reshape(
            2, heads, 1, dim
        )
        for name, at in sections.items()
    }
    docs = {"f": fwd_docs, "b": bwd_docs}
    ins, outs = plan
    latest, where = None, {}
    for pieces in ins:
        latest = exchange(after(pack(sources, pieces, ranks, dim), latest))
        for (name, head), first in places(pieces, KINDS_IN)[0].items():
            where.setdefault(name, (latest, []))[1].append((head, first))
    held, earlier = {}, None
    for names in outs:
        out, base = (), 0
        kinds = sum(KINDS_OUT[name] for name in names) * heads
        for name in names:
            group, pieces = where[name]
            results, *new = attend(
                name, after(group, earlier), tuple(pieces), gains[name], docs[name], kinds, base, out,
                len(ins) == 1 or group is not latest,
            )
            if new:
                up_local = accum[1] + new[0].reshape(accum[1].shape)
                mirrored = lax.ppermute(up_local, "pipe", mirror)
                total = lax.psum(accum[0] + mirrored, "dp")
            out, earlier = (results,), results
            base += KINDS_OUT[name] * heads
        latest = exchange(after(results, (latest, total) if held.get("b") is not None else latest))
        held.update(zip(names, unpack(latest, names, heads)))
    return held["b"], held["f"], into_hbm(total)


def body(fwd_qkv, bwd_qkv, bwd_grad_out, fwd_doc, bwd_doc, norm_gain, grad_acc):
    ranks = lax.axis_size("head")
    pipe_count = lax.axis_size("pipe")
    pipe_at = lax.axis_index("pipe")
    tokens = fwd_qkv.shape[2]
    width = fwd_qkv.shape[4]
    dim = norm_gain.shape[3]
    local_heads = norm_gain.shape[2] // ranks

    args = (
        fwd_qkv.reshape(tokens, 3, width).transpose(1, 0, 2),
        bwd_qkv.reshape(tokens, 3, width).transpose(1, 0, 2),
        bwd_grad_out.reshape(1, tokens, width),
        norm_gain,
        fwd_doc.reshape(-1, LANES),
        bwd_doc.reshape(-1, LANES),
        grad_acc.reshape(2, 2, local_heads, dim),
    )
    plans = [(at ^ (at >> 1)) & 1 for at in range(pipe_count)]
    mirrors = [
        [(at, pipe_count - 1 - at) for at in range(pipe_count) if plans[at] == plan]
        for plan in range(2)
    ]
    qkv_grad, fwd_out, total = lax.cond(
        (pipe_at ^ (pipe_at >> 1)) & 1 == 0,
        functools.partial(branch, PLANS[0], mirrors[0]),
        functools.partial(branch, PLANS[1], mirrors[1]),
        *args,
    )
    return (
        fwd_out.reshape(1, 1, tokens, width),
        qkv_grad.transpose(1, 0, 2).reshape(1, 1, tokens, 3, width),
        total.reshape(1, 2, local_heads, dim),
    )


def solution(mesh):
    in_specs = (
        P("dp", "pipe", "head", None, None),
        P("dp", "pipe", "head", None, None),
        P("dp", "pipe", "head", None),
        P("dp", "pipe", None),
        P("dp", "pipe", None),
        P(),
        P("dp", "pipe", None, None, "head", None),
    )
    out_specs = (
        P("dp", "pipe", "head", None),
        P("dp", "pipe", "head", None, None),
        P("pipe", None, "head", None),
    )
    return jax.shard_map(body, mesh=mesh, in_specs=in_specs, out_specs=out_specs, check_vma=False)
```
